32 devices in a mesh: dx: 4 (over z), dy: 8 (over y, x, core).
Axes of the slice: x: 2, y: 2, z: 4, core: 2. Of those that a mesh axis runs over, the one named last changes fastest.
Arguments:
- dust: bfloat16 [131072, 256], P(('dx', 'dy')), may hold values from 0.19921875 to 2
- classes: int32 [131072], P(('dx', 'dy')), may hold values from 0 to 7
- kernels: bfloat16 [8, 2, 128, 128], replicated, may hold values from -0.5 to 0.5
- export_ids: int32 [32, 4, 1024], P(('dx', 'dy')), may hold values from 0 to 4095
- faces: int32 [6, 131072], P(None, ('dx', 'dy')), may hold values from 0 to 8191, as said below
- face_coef: float32 [6, 131072], P(None, ('dx', 'dy')), may hold values from 0.04 to 0.16
- mig_ids: int32 [1024, 16], P(('dx', 'dy')), may hold values from 0 to 4095, as said below
- mig_counts: int32 [32, 32], P(('dx', 'dy')), may hold values from 0 to 16, as said below
Outputs:
- dust_next: bfloat16 [131072, 256], P(('dx', 'dy'))
- arrivals: bfloat16 [16384, 256], P(('dx', 'dy'))
The draws below stay inside these ranges and needn't reach their ends.
Inputs may be any that keep to these rules, and one draw needn't show every extreme that they name: Entries below 4096 name cells of the same domain, entries from 4096 on name its received rows in the order of the steps; each cell has 4 to 6 faces and its other slots name the cell itself. `mig_ids`: the 512 entries of one domain's rows are distinct local cells. `mig_counts`: one destination, drawn from the seed, receives 16 cells from every domain.
All inputs are finite; a program needn't handle non-finite values.
Results may differ from the reference program's by a relative error of at most 0.0054.
Values may be sent and summed in bfloat16 or wider, within the bound.
No kernel may reach another device: no remote copies, remote signals or barrier semaphores. Data moves between devices by JAX's collectives and lax.ppermute only.
A program may use at most 64 MiB of HBM per device.

```python
import math
import jax
import jax.numpy as jnp
from jax import lax

B = 128
S = 2
NCLASS = 8
NFACE = 6
SUBSTEPS = 6
CAP = 16
CELLS_DEV = 4096
EXP = 1024
NDEV = 32
CELLS = 131072
N_DX = 4
N_DY = 8


def draw_faces(key, part):
    key_count, key_local, key_ghost, key_choose = jax.random.split(key, 4)
    own_index = jnp.arange(CELLS, dtype=jnp.int32) % CELLS_DEV
    real_count = jax.random.randint(key_count, (CELLS,), 4, NFACE + 1)
    slot_number = jnp.arange(NFACE, dtype=jnp.int32)[:, None]
    local_target = jax.random.randint(key_local, (NFACE, CELLS), 0, CELLS_DEV)
    ghost_target = CELLS_DEV + jax.random.randint(key_ghost, (NFACE, CELLS), 0, 4 * EXP)
    chooser = jax.random.randint(key_choose, (NFACE, CELLS), 0, 10)
    target = jnp.where(chooser == 0, ghost_target, local_target)
    return jnp.where(slot_number < real_count[None, :], target, own_index[None, :]).astype(jnp.int32)


def draw_mig_ids(key, part):
    domain_keys = jax.random.split(key, NDEV)

    def permuted(domain_key):
        return jax.random.permutation(domain_key, CELLS_DEV)[:NDEV * CAP].astype(jnp.int32)
    return jax.vmap(permuted)(domain_keys).reshape(NDEV * NDEV, CAP)


def draw_mig_counts(key, part):
    key_base, key_target = jax.random.split(key)
    base_counts = jax.random.randint(key_base, (NDEV, NDEV), 0, CAP + 1)
    busiest = jax.random.randint(key_target, (), 0, NDEV)
    column = jnp.arange(NDEV, dtype=jnp.int32)[None, :]
    return jnp.where(column == busiest, CAP, base_counts).astype(jnp.int32)


def touch_ends(drawn, key, smallest, top_value):
    index_at = [jax.random.randint(jax.random.fold_in(key, axis), (), 0, length) for axis, length in enumerate(drawn.shape)]
    widest = drawn.shape.index(max(drawn.shape))
    beside = index_at[:widest] + [(index_at[widest] + 1) % drawn.shape[widest]] + index_at[widest + 1:]
    return drawn.at[tuple(index_at)].set(smallest).at[tuple(beside)].set(top_value)


def block_levels(key, shape, cuts, least, high):
    def one(axis_at, parts):
        draws = jax.random.uniform(jax.random.fold_in(jax.random.fold_in(key, 6), axis_at), (parts,), jnp.float32, least / len(cuts), high / len(cuts))
        return jnp.repeat(jnp.exp(draws), shape[axis_at] // parts).reshape((-1,) + (1,) * (len(shape) - axis_at - 1))

    level = one(*cuts[0])
    for cut in cuts[1:]:
        level = level * one(*cut)
    return level


def scatter_about(rng, extent, scale, limit, kind=jnp.bfloat16):
    result = scale * jax.random.normal(rng, extent, jnp.float32)
    return jnp.clip(result, min=-limit, max=limit).astype(kind)


def setup_inputs(seed: int = 0) -> dict:
    seeds = jax.random.split(jax.random.key(seed), 9)
    dust = jnp.clip(0.19921875 + 1.8007812 * jax.random.uniform(seeds[0], (CELLS, S * B), jnp.float32) ** block_levels(seeds[0], (CELLS, S * B), ((0, 32),), -0.2, 0.2), 0.19921875, 2.0).astype(jnp.bfloat16)
    classes = touch_ends(jax.random.randint(seeds[1], (CELLS,), 0, NCLASS), jax.random.fold_in(seeds[1], 1), 0, NCLASS - 1).astype(jnp.int32)
    kernels = scatter_about(seeds[2], (NCLASS, S, B, B), B ** -0.5, 0.5)
    export_ids = touch_ends(jax.random.randint(seeds[3], (NDEV, 4, EXP), 0, CELLS_DEV), jax.random.fold_in(seeds[3], 1), 0, CELLS_DEV - 1).astype(jnp.int32)
    faces = draw_faces(jax.random.fold_in(seeds[8], 71), 0)
    face_coef = jnp.clip(jnp.exp(math.log(0.16) - 1.3862944 * jax.random.uniform(seeds[5], (NFACE, CELLS), jnp.float32) ** block_levels(seeds[5], (NFACE, CELLS), ((1, 32),), -0.2, 0.2)), 0.04, 0.16)
    mig_ids = draw_mig_ids(jax.random.fold_in(seeds[8], 71), 0)
    mig_counts = draw_mig_counts(jax.random.fold_in(seeds[8], 71), 0)
    return dict(dust=dust, classes=classes, kernels=kernels, export_ids=export_ids, faces=faces, face_coef=face_coef, mig_ids=mig_ids, mig_counts=mig_counts)


def coagulate(dust_rows, dust_classes, kernels):
    row_count = dust_rows.shape[0]
    sort_order = jnp.argsort(dust_classes, stable=True).astype(jnp.int32)
    sorted_rows = jnp.take(dust_rows, sort_order, axis=0)
    sorted_classes = jnp.take(dust_classes, sort_order, axis=0)
    block_rows = 2048 if row_count % 2048 == 0 else row_count
    block_count = row_count // block_rows

    def run_block(pieces):
        piece_rows, piece_classes = pieces
        lowest = piece_classes[0]
        highest = piece_classes[block_rows - 1]
        grain_state = piece_rows.astype(jnp.float32).reshape(block_rows, S, B)
        for substep in range(SUBSTEPS):
            operand = lax.optimization_barrier(grain_state.astype(jnp.bfloat16)).astype(jnp.float32)

            def add_class(class_id, product):
                kernel = lax.dynamic_index_in_dim(kernels, class_id, 0, keepdims=False).astype(jnp.float32)
                partial_value = jnp.einsum("rsb,sbc->rsc", operand, kernel)
                return jnp.where((piece_classes == class_id)[:, None, None], partial_value, product)

            product = lax.fori_loop(lowest, highest + 1, add_class, jnp.zeros((block_rows, S, B), jnp.float32))
            mean_square = jnp.mean(grain_state * grain_state, axis=2, keepdims=True)
            grain_state = grain_state + product * (mean_square / (1.0 + mean_square))
        return grain_state.reshape(block_rows, S * B).astype(jnp.bfloat16)

    blocked = lax.map(run_block, (sorted_rows.reshape(block_count, block_rows, S * B), sorted_classes.reshape(block_count, block_rows)))
    inverse = jnp.zeros((row_count,), jnp.int32).at[sort_order].set(jnp.arange(row_count, dtype=jnp.int32))
    return jnp.take(blocked.reshape(row_count, S * B), inverse, axis=0)


def reference(dust, classes, kernels, export_ids, faces, face_coef, mig_ids, mig_counts):
    devices = N_DX * N_DY
    cells_local = dust.shape[0] // devices
    row_width = S * B
    coag = coagulate(dust, classes, kernels)
    domain_rows = coag.reshape(N_DX, N_DY, cells_local, row_width)
    export_rows = export_ids.reshape(N_DX, N_DY, 4 * EXP)

    def pick_rows(source, index):
        return jnp.take(source, index, axis=0)

    outbound = jax.vmap(jax.vmap(pick_rows))(domain_rows, export_rows).reshape(N_DX, N_DY, 4, EXP, row_width)
    ghosts = jnp.stack([
        jnp.roll(outbound[:, :, 0], 1, axis=0),
        jnp.roll(outbound[:, :, 1], -1, axis=0),
        jnp.roll(outbound[:, :, 2], 1, axis=1),
        jnp.roll(outbound[:, :, 3], -1, axis=1)], axis=2).reshape(N_DX, N_DY, 4 * EXP, row_width)
    extended = jnp.concatenate([domain_rows, ghosts], axis=2).reshape(devices, cells_local + 4 * EXP, row_width)
    local_faces = faces.reshape(NFACE, devices, cells_local).transpose(1, 0, 2)
    local_coefs = face_coef.reshape(NFACE, devices, cells_local).transpose(1, 0, 2)

    def diffuse(pieces):
        extended_rows, face_rows, coefs = pieces
        own_rows = extended_rows[:cells_local].astype(jnp.float32)
        flux_sum = own_rows
        for face in range(NFACE):
            neighbour = jnp.take(extended_rows, face_rows[face], axis=0).astype(jnp.float32)
            flux_sum = flux_sum + coefs[face][:, None] * (neighbour - own_rows)
        return flux_sum.astype(jnp.bfloat16)

    updated = lax.map(diffuse, (extended, local_faces, local_coefs))
    slot_index = mig_ids.reshape(devices, devices, CAP)
    filled = jnp.arange(CAP, dtype=jnp.int32)[None, None, :] < mig_counts[:, :, None]

    def pack(pieces):
        source_rows, index, valid = pieces
        picked = jnp.take(source_rows, index.reshape(devices * CAP), axis=0).reshape(devices, CAP, row_width)
        return jnp.where(valid[:, :, None], picked, jnp.zeros_like(picked))

    leaving = lax.map(pack, (updated, slot_index, filled))
    arrivals = leaving.transpose(1, 0, 2, 3).reshape(devices * devices * CAP, row_width)
    return updated.reshape(devices * cells_local, row_width), arrivals
```

```python
import functools

import jax
import jax.numpy as jnp
from jax import lax
from jax.experimental import pallas as pl
from jax.experimental.pallas import tpu as pltpu
from jax.sharding import PartitionSpec as P

SUBSTEPS = 6
LANES = 128
GROUP = 8
TILE = 128
TOGETHER = 4
CHUNK = 16
F32 = jnp.float32
BF16 = jnp.bfloat16
I32 = jnp.int32
MIB = 1 << 20


def passed_along(block, axis, distance):
    devices = range(lax.axis_size(axis))
    route = [((i - distance) % len(devices), i) for i in devices]
    return lax.ppermute(block, axis, route)


def iota2(shape, dim):
    return lax.broadcasted_iota(I32, shape, dim)


def dot(a, b):
    return jnp.dot(a, b, preferred_element_type=F32)


def rows2(start):
    return pl.ds(pl.multiple_of(start, 2), 2)


def spread_rows(src, table, first, count):
    step = 64

    def one(i, carry):
        block = src[pl.ds(pl.multiple_of(i * step, step), step), :].astype(F32)
        at = 2 * first + i * (2 * step)
        table[pl.ds(pl.multiple_of(at, 8), step, stride=2), :] = block[:, :LANES]
        table[pl.ds(at + 1, step, stride=2), :] = block[:, LANES:]
        return carry

    lax.fori_loop(0, count // step, one, 0)


def class_places(cls, class_count, tile):
    rows = cls.shape[0]
    shift = rows.bit_length() - 1
    wide = class_count * rows
    member = jnp.concatenate([(cls == c).astype(F32) for c in range(class_count)], axis=0)
    member16 = member.astype(BF16)
    before = (iota2((LANES, LANES), 0) < iota2((LANES, LANES), 1)).astype(F32).astype(BF16)
    in_row = dot(member16, before)
    row_total = dot(member16, jnp.ones((LANES, LANES), BF16)).astype(BF16)
    a, b = iota2((wide, wide), 0), iota2((wide, wide), 1)
    same = (a >> shift) == (b >> shift)
    earlier_rows = jnp.logical_and(same, b < a).astype(F32).astype(BF16)
    row_start = dot(earlier_rows, row_total)
    class_total = dot(same.astype(F32).astype(BF16), row_total)
    tiles = ((class_total.astype(I32) + (tile - 1)) >> (tile.bit_length() - 1)).astype(F32)
    earlier = jnp.logical_and((b >> shift) < (a >> shift), (b & (rows - 1)) == 0)
    first_tile = dot(earlier.astype(F32).astype(BF16), tiles.astype(BF16))
    place = member * (first_tile * float(tile) + row_start + in_row)
    total = place[:rows]
    for c in range(1, class_count):
        total = total + place[c * rows:(c + 1) * rows]
    last_tile = (first_tile + tiles).astype(I32)
    lane = iota2((8, LANES), 1)
    tile_class = jnp.zeros((8, LANES), I32)
    for c in range(class_count - 1):
        tile_class = tile_class + (last_tile[c * rows:c * rows + 8] <= lane).astype(I32)
    tile_count = last_tile[wide - 8:]
    return (2.0 * total).astype(I32), tile_class, tile_count


def substeps(state, weights, averager):
    for _ in range(SUBSTEPS):
        operand = state.astype(BF16)
        product = dot(operand, weights)
        mean_square = dot(operand * operand, averager)
        share = pl.reciprocal(1.0 + mean_square, approx=True)
        state = state + product * (1.0 - share)
    return state


def own_kernel(cells, cls_ref, step_ref, exp_ref, dust, kern, out, outbound, table, sorted_rows, weights, averager,
               places_v, places, stage, sem):
    class_count = kern.shape[0]
    rows = cells // LANES
    place, tile_class, tile_count = class_places(cls_ref[...], class_count, TILE)
    places_v[0:rows, :] = place
    places_v[rows:rows + 8, :] = tile_class
    places_v[rows + 8:rows + 16, :] = tile_count
    copy = pltpu.make_async_copy(places_v, places, sem)
    copy.start()
    spread_rows(dust, table, 0, cells)
    zero = jnp.zeros((LANES, LANES), BF16)
    mean = jnp.full((LANES, LANES), 1.0 / LANES, BF16)
    for s in range(2):
        averager[s * LANES:(s + 1) * LANES, s * LANES:(s + 1) * LANES] = mean
        averager[s * LANES:(s + 1) * LANES, (1 - s) * LANES:(2 - s) * LANES] = zero
    for c in range(class_count):
        for s in range(2):
            weights[c, s * LANES:(s + 1) * LANES, s * LANES:(s + 1) * LANES] = kern[c, s]
            weights[c, s * LANES:(s + 1) * LANES, (1 - s) * LANES:(2 - s) * LANES] = zero
    steps = [step_ref[k] for k in range(GROUP)]
    copy.wait()

    def scatter(r, carry):
        for j in range(LANES // GROUP):
            group = places.at[r, pl.ds(j * GROUP, GROUP)]
            for k in range(GROUP):
                at = (r * LANES + j * GROUP + k) * 2
                sorted_rows[rows2(group[steps[k]]), :] = table[rows2(at), :]
        return carry

    lax.fori_loop(0, rows, scatter, 0)
    total_tiles = places[rows + 8, 0]

    def tiles(i, carry):
        states, firsts = [], []
        for m in range(TOGETHER):
            first = (i * TOGETHER + m) * (2 * TILE)
            one = sorted_rows[pl.ds(pl.multiple_of(first, 8), TILE, stride=2), :]
            two = sorted_rows[pl.ds(first + 1, TILE, stride=2), :]
            states.append(jnp.concatenate([one, two], axis=1))
            firsts.append(first)
        mats = [weights[jnp.minimum(places[rows, i * TOGETHER + m], class_count - 1)] for m in range(TOGETHER)]
        avg = averager[...]
        for m in range(TOGETHER):
            done = substeps(states[m], mats[m], avg).astype(BF16).astype(F32)
            sorted_rows[pl.ds(pl.multiple_of(firsts[m], 8), TILE, stride=2), :] = done[:, :LANES]
            sorted_rows[pl.ds(firsts[m] + 1, TILE, stride=2), :] = done[:, LANES:]
        return carry

    lax.fori_loop(0, (total_tiles + (TOGETHER - 1)) // TOGETHER, tiles, 0)

    def gather(r, carry):
        for j in range(LANES // GROUP):
            group = places.at[r, pl.ds(j * GROUP, GROUP)]
            for k in range(GROUP):
                at = (r * LANES + j * GROUP + k) * 2
                out[rows2(at), :] = sorted_rows[rows2(group[steps[k]]), :]
        return carry

    lax.fori_loop(0, rows, gather, 0)
    export = outbound.shape[0]
    span = 64

    def send(i, carry):
        for j in range(span // GROUP):
            group = exp_ref.at[pl.ds(i * span + j * GROUP, GROUP)]
            for k in range(GROUP):
                stage[rows2((j * GROUP + k) * 2), :] = out[rows2(group[steps[k]]), :]
        at = pl.ds(pl.multiple_of(i * span, span), span)
        outbound[at, 0:LANES] = stage[pl.ds(0, span, stride=2), :].astype(BF16)
        outbound[at, LANES:2 * LANES] = stage[pl.ds(1, span, stride=2), :].astype(BF16)
        return carry

    lax.fori_loop(0, export // span, send, 0)


def vmem():
    return pl.BlockSpec(memory_space=pltpu.VMEM)


def smem():
    return pl.BlockSpec(memory_space=pltpu.SMEM)


def own_cells(dust, classes, kernels, export2, steps):
    cells = dust.shape[0]
    rows = cells // LANES
    class_count = kernels.shape[0]
    most = (cells // TILE + class_count + TOGETHER - 1) // TOGETHER * TOGETHER
    return pl.pallas_call(
        functools.partial(own_kernel, cells),
        out_shape=(
            jax.ShapeDtypeStruct((2 * cells, LANES), F32),
            jax.ShapeDtypeStruct((export2.shape[0], 2 * LANES), BF16),
        ),
        in_specs=[vmem(), smem(), smem(), vmem(), vmem()],
        out_specs=(vmem(), vmem()),
        scratch_shapes=[
            pltpu.VMEM((2 * cells, LANES), F32),
            pltpu.VMEM((2 * most * TILE, LANES), F32),
            pltpu.VMEM((class_count, 2 * LANES, 2 * LANES), BF16),
            pltpu.VMEM((2 * LANES, 2 * LANES), BF16),
            pltpu.VMEM((rows + 16, LANES), I32),
            pltpu.SMEM((rows + 16, LANES), I32),
            pltpu.VMEM((128, LANES), F32),
            pltpu.SemaphoreType.DMA,
        ],
        compiler_params=pltpu.CompilerParams(vmem_limit_bytes=40 * MIB),
        cost_estimate=pl.CostEstimate(flops=9_000_000_000, bytes_accessed=12 * MIB, transcendentals=0),
        name="coagulate_own",
    )(classes.reshape(rows, LANES), steps, export2, dust, kernels)


def fill_table(own, ghosts, table, sem):
    cells2 = own.shape[0]
    copy = pltpu.make_async_copy(own, table.at[pl.ds(0, cells2)], sem)
    copy.start()
    first = cells2 // 2
    for ghost in ghosts:
        spread_rows(ghost, table, first, ghost.shape[0])
        first = first + ghost.shape[0]
    copy.wait()


def diffused(own1, own2, coef, stage, face_count):
    one, two = own1, own2
    for f in range(face_count):
        c = jnp.broadcast_to(coef[:, f:f + 1], (CHUNK, LANES))
        one = one + c * (stage[pl.ds(2 * f * CHUNK, CHUNK, stride=2), :] - own1)
        two = two + c * (stage[pl.ds(2 * f * CHUNK + 1, CHUNK, stride=2), :] - own2)
    return one.astype(BF16), two.astype(BF16)


def mig_kernel(face_count, cells, faces, mig, own, g0, g1, g2, g3, coef, out, table, stage, own_stage, coef_stage, sem):
    fill_table(own, (g0, g1, g2, g3), table, sem)

    def chunk(i, carry):
        for u in range(CHUNK):
            c = mig[i * CHUNK + u]
            own_stage[rows2(2 * u), :] = table[rows2(2 * c), :]
            coef_stage[pl.ds(u, 1), :] = coef[pl.ds(c, 1), :]
            for f in range(face_count):
                row = faces.at[pl.ds(f * cells, cells)][c]
                stage[rows2((f * CHUNK + u) * 2), :] = table[rows2(row), :]
        one, two = diffused(own_stage[pl.ds(0, CHUNK, stride=2), :], own_stage[pl.ds(1, CHUNK, stride=2), :],
                            coef_stage[...], stage, face_count)
        at = pl.ds(pl.multiple_of(i * CHUNK, CHUNK), CHUNK)
        out[at, 0:LANES] = one
        out[at, LANES:2 * LANES] = two
        return carry

    lax.fori_loop(0, out.shape[0] // CHUNK, chunk, 0)


def all_kernel(face_count, cells, faces, steps_ref, own, g0, g1, g2, g3, coef, out, table, stage_a, stage_b, sem):
    fill_table(own, (g0, g1, g2, g3), table, sem)
    steps = [steps_ref[k] for k in range(GROUP)]

    def pull(i, stage):
        for f in range(face_count):
            for j in range(CHUNK // GROUP):
                group = faces.at[pl.ds(i * CHUNK + (f * cells + j * GROUP), GROUP)]
                for k in range(GROUP):
                    stage[rows2((f * CHUNK + j * GROUP + k) * 2), :] = table[rows2(group[steps[k]]), :]

    def push(i, stage):
        first = i * (2 * CHUNK)
        one, two = diffused(
            table[pl.ds(pl.multiple_of(first, 8), CHUNK, stride=2), :],
            table[pl.ds(first + 1, CHUNK, stride=2), :],
            coef[pl.ds(pl.multiple_of(i * CHUNK, CHUNK), CHUNK), :], stage, face_count)
        at = pl.ds(pl.multiple_of(i * CHUNK, CHUNK), CHUNK)
        out[at, 0:LANES] = one
        out[at, LANES:2 * LANES] = two

    pull(0, stage_a)
    chunks = cells // CHUNK

    def pair(i, carry):
        push(2 * i, stage_a)
        pull(2 * i + 1, stage_b)
        push(2 * i + 1, stage_b)
        pull(jnp.minimum(2 * i + 2, chunks - 1), stage_a)
        return carry

    lax.fori_loop(0, chunks // 2, pair, 0)


def diffuse_leaving(faces2, mig, own, ghosts, coef, face_count):
    cells = own.shape[0] // 2
    ghost_rows = sum(g.shape[0] for g in ghosts)
    return pl.pallas_call(
        functools.partial(mig_kernel, face_count, cells),
        out_shape=jax.ShapeDtypeStruct((mig.shape[0], 2 * LANES), BF16),
        in_specs=[smem(), smem(), pl.BlockSpec(memory_space=pl.ANY)] + [vmem()] * 5,
        out_specs=vmem(),
        scratch_shapes=[
            pltpu.VMEM((2 * (cells + ghost_rows), LANES), F32),
            pltpu.VMEM((2 * face_count * CHUNK, LANES), F32),
            pltpu.VMEM((2 * CHUNK, LANES), F32),
            pltpu.VMEM((CHUNK, face_count), F32),
            pltpu.SemaphoreType.DMA,
        ],
        compiler_params=pltpu.CompilerParams(vmem_limit_bytes=30 * MIB),
        cost_estimate=pl.CostEstimate(flops=500_000_000, bytes_accessed=8 * MIB, transcendentals=0),
        name="diffuse_leaving",
    )(faces2, mig, own, *ghosts, coef)


def diffuse_all(faces2, steps, own, ghosts, coef, face_count):
    cells = own.shape[0] // 2
    ghost_rows = sum(g.shape[0] for g in ghosts)
    return pl.pallas_call(
        functools.partial(all_kernel, face_count, cells),
        out_shape=jax.ShapeDtypeStruct((cells, 2 * LANES), BF16),
        in_specs=[smem(), smem(), pl.BlockSpec(memory_space=pl.ANY)] + [vmem()] * 5,
        out_specs=vmem(),
        scratch_shapes=[
            pltpu.VMEM((2 * (cells + ghost_rows), LANES), F32),
            pltpu.VMEM((2 * face_count * CHUNK, LANES), F32),
            pltpu.VMEM((2 * face_count * CHUNK, LANES), F32),
            pltpu.SemaphoreType.DMA,
        ],
        compiler_params=pltpu.CompilerParams(vmem_limit_bytes=30 * MIB),
        cost_estimate=pl.CostEstimate(flops=10_000_000_000, bytes_accessed=30 * MIB, transcendentals=0),
        name="diffuse_all",
    )(faces2, steps, own, *ghosts, coef)


def body(dust, classes, kernels, export_ids, faces, face_coef, mig_ids, mig_counts):
    row_width = dust.shape[1]
    face_count = faces.shape[0]
    export_count = export_ids.shape[2]
    steps = jnp.arange(GROUP, dtype=I32)
    export2 = (export_ids * 2).reshape(4 * export_count)
    own, outbound = own_cells(dust, classes, kernels, export2, steps)
    blocks = outbound.reshape(4, export_count, row_width)
    ghosts = []
    for direction, offset in ((0, 1), (1, -1)):
        ghosts.append(passed_along(blocks[direction], "dx", offset))
    for direction, offset in ((2, 1), (3, -1)):
        ghosts.append(passed_along(blocks[direction], "dy", offset))
    faces2 = (faces * 2).reshape(-1)
    coef = face_coef.T
    domains = mig_counts.shape[1]
    capacity = mig_ids.shape[1]
    picked = diffuse_leaving(faces2, mig_ids.reshape(-1), own, ghosts, coef, face_count)
    filled = jnp.arange(capacity, dtype=I32)[None, :] < mig_counts[0][:, None]
    picked = picked.reshape(domains, capacity, row_width)
    leaving = jnp.where(filled[:, :, None], picked, jnp.zeros_like(picked))
    arrived = lax.all_to_all(leaving, ("dx", "dy"), split_axis=0, concat_axis=0, tiled=True)
    updated = diffuse_all(faces2, steps, own, ghosts, coef, face_count)
    return (updated, arrived.reshape(domains * capacity, row_width))


def solution(mesh):
    return jax.shard_map(
        body,
        mesh=mesh,
        in_specs=(
            P(("dx", "dy"), None),
            P(("dx", "dy")),
            P(),
            P(("dx", "dy"), None, None),
            P(None, ("dx", "dy")),
            P(None, ("dx", "dy")),
            P(("dx", "dy"), None),
            P(("dx", "dy"), None),
        ),
        out_specs=(P(("dx", "dy"), None), P(("dx", "dy"), None)),
        check_vma=False,
    )
```

```python
import functools

import jax
import jax.numpy as jnp
from jax import lax
from jax.experimental import pallas as pl
from jax.experimental.pallas import tpu as pltpu
from jax.sharding import PartitionSpec as P

SUBSTEPS = 6
LANES = 128
GROUP = 8
TILE = 576
CHUNK = 16
F32 = jnp.float32
BF16 = jnp.bfloat16
I32 = jnp.int32
MIB = 1 << 20
VMEM_MIB = 60


def passed_along(block, axis, distance):
    devices = range(lax.axis_size(axis))
    route = [((i - distance) % len(devices), i) for i in devices]
    return lax.ppermute(block, axis, route)


def iota2(shape, dim):
    return lax.broadcasted_iota(I32, shape, dim)


def small_numbers(none_negative):
    unit = jnp.minimum(none_negative, 0) + 1
    return [unit * k for k in range(GROUP)]


def lines_of(source, lines, times):
    per_row = source.shape[1] // LANES
    for r in range(source.shape[0]):
        for i in range(per_row):
            at = r * per_row + i
            lines[at:at + 1, :] = source[r:r + 1, i * LANES:(i + 1) * LANES] * times


def dot(a, b):
    return jnp.dot(a, b, preferred_element_type=F32)


def rows2(start):
    return pl.ds(pl.multiple_of(start, 2), 2)


def spread_rows(src, table, first, count):
    step = 256

    def one(i, carry):
        block = src[pl.ds(pl.multiple_of(i * step, step), step), :].astype(F32)
        at = 2 * first + i * (2 * step)
        table[pl.ds(pl.multiple_of(at, 8), step, stride=2), :] = block[:, :LANES]
        table[pl.ds(at + 1, step, stride=2), :] = block[:, LANES:]
        return carry

    lax.fori_loop(0, count // step, one, 0)


def class_places(cls, class_count, tile):
    rows = cls.shape[0]
    shift = rows.bit_length() - 1
    wide = class_count * rows
    member = jnp.concatenate([(cls == c).astype(F32) for c in range(class_count)], axis=0)
    member16 = member.astype(BF16)
    before = (iota2((LANES, LANES), 0) < iota2((LANES, LANES), 1)).astype(F32).astype(BF16)
    in_row = dot(member16, before)
    row_total = dot(member16, jnp.ones((LANES, LANES), BF16)).astype(BF16)
    a, b = iota2((wide, wide), 0), iota2((wide, wide), 1)
    same = (a >> shift) == (b >> shift)
    earlier_rows = jnp.logical_and(same, b < a).astype(F32).astype(BF16)
    row_start = dot(earlier_rows, row_total)
    class_total = dot(same.astype(F32).astype(BF16), row_total)
    tiles = ((class_total + (tile - 0.5)) * (1.0 / tile)).astype(I32).astype(F32)
    earlier = jnp.logical_and((b >> shift) < (a >> shift), (b & (rows - 1)) == 0)
    first_tile = dot(earlier.astype(F32).astype(BF16), tiles.astype(BF16))
    place = member * (first_tile * float(tile) + row_start + in_row)
    total = place[:rows]
    for c in range(1, class_count):
        total = total + place[c * rows:(c + 1) * rows]
    last_tile = (first_tile + tiles).astype(I32)
    lane = iota2((8, LANES), 1)
    tile_class = jnp.zeros((8, LANES), I32)
    for c in range(class_count - 1):
        tile_class = tile_class + (last_tile[c * rows:c * rows + 8] <= lane).astype(I32)
    tile_count = last_tile[wide - 8:]
    return (2.0 * total).astype(I32), tile_class, tile_count


def substeps(state, weights):
    one, two = state[:, :LANES], state[:, LANES:]
    bins = float(LANES)
    for _ in range(SUBSTEPS):
        operand = jnp.concatenate([one, two], axis=1).astype(BF16)
        square_one = jnp.sum(one * one, axis=1, keepdims=True)
        square_two = jnp.sum(two * two, axis=1, keepdims=True)
        product = dot(operand, weights)
        one = one + product[:, :LANES] * (1.0 / bins - pl.reciprocal(bins + square_one, approx=True))
        two = two + product[:, LANES:] * (1.0 / bins - pl.reciprocal(bins + square_two, approx=True))
    return one.astype(BF16), two.astype(BF16)


def send_rows(ids, line, steps, table, outbound, stages):
    span = stages[0].shape[0] // 2
    spans = outbound.shape[0] // span

    def pull(i, stage):
        for j in range(span // GROUP):
            group = ids.at[line + i, pl.ds(j * GROUP, GROUP)]
            for k in range(GROUP):
                stage[rows2((j * GROUP + k) * 2), :] = table[rows2(group[steps[k]]), :]

    def push(i, stage):
        at = pl.ds(pl.multiple_of(i * span, span), span)
        outbound[at, 0:LANES] = stage[pl.ds(0, span, stride=2), :].astype(BF16)
        outbound[at, LANES:2 * LANES] = stage[pl.ds(1, span, stride=2), :].astype(BF16)

    pull(0, stages[0])

    def pair(i, carry):
        push(2 * i, stages[0])
        pull(2 * i + 1, stages[1])
        push(2 * i + 1, stages[1])
        pull(jnp.minimum(2 * i + 2, spans - 1), stages[0])
        return carry

    lax.fori_loop(0, spans // 2, pair, 0)


def own_kernel(cells, cls_ref, exp_ref, dust_any, kern_any, out_any, out_up, out_down, out_left, out_right,
               out, dust, kern, sorted_rows, weights, places_v, places, exp_v, exp_s, stage_a, stage_b, sem, dust_sems, kern_sem, exp_sem):
    class_count = kern.shape[0]
    rows = cells // LANES
    parts = dust_sems.shape[0]
    part = cells // parts
    kern_copy = pltpu.make_async_copy(kern_any, kern, kern_sem)
    kern_copy.start()
    dust_copies = []
    for p in range(parts):
        at = pl.ds(p * part, part)
        dust_copies.append(pltpu.make_async_copy(dust_any.at[at], dust.at[at], dust_sems.at[p]))
        dust_copies[-1].start()
    export_lines = exp_ref.shape[2] // LANES
    lines_of(exp_ref.at[0], exp_v, 2)
    exp_copy = pltpu.make_async_copy(exp_v, exp_s, exp_sem)
    exp_copy.start()
    place, tile_class, tile_count = class_places(cls_ref[...], class_count, TILE)
    places_v[0:rows, :] = place
    places_v[rows:rows + 8, :] = tile_class
    places_v[rows + 8:rows + 16, :] = tile_count
    copy = pltpu.make_async_copy(places_v, places, sem)
    copy.start()
    zero = jnp.zeros((LANES, LANES), BF16)
    kern_copy.wait()
    for c in range(class_count):
        for s in range(2):
            own = kern[c, s].astype(F32) * float(LANES)
            weights[c, s * LANES:(s + 1) * LANES, s * LANES:(s + 1) * LANES] = own.astype(BF16)
            weights[c, s * LANES:(s + 1) * LANES, (1 - s) * LANES:(2 - s) * LANES] = zero
    for dust_copy in dust_copies:
        dust_copy.wait()
    copy.wait()
    exp_copy.wait()
    steps = small_numbers(places[0, 0])

    def widen(r, stage):
        block = dust[pl.ds(pl.multiple_of(r * LANES, LANES), LANES), :].astype(F32)
        stage[pl.ds(0, LANES, stride=2), :] = block[:, :LANES]
        stage[pl.ds(1, LANES, stride=2), :] = block[:, LANES:]

    def scatter(r, stage):
        for j in range(LANES // GROUP):
            group = places.at[r, pl.ds(j * GROUP, GROUP)]
            for k in range(GROUP):
                sorted_rows[rows2(group[steps[k]]), :] = stage[rows2((j * GROUP + k) * 2), :]

    widen(0, stage_a)

    def pair(i, carry):
        scatter(2 * i, stage_a)
        widen(2 * i + 1, stage_b)
        scatter(2 * i + 1, stage_b)
        widen(jnp.minimum(2 * i + 2, rows - 1), stage_a)
        return carry

    lax.fori_loop(0, rows // 2, pair, 0)

    def tile(i, carry):
        first = i * (2 * TILE)
        at_one = pl.ds(pl.multiple_of(first, 8), TILE, stride=2)
        at_two = pl.ds(first + 1, TILE, stride=2)
        state = jnp.concatenate([sorted_rows[at_one, :], sorted_rows[at_two, :]], axis=1)
        one, two = substeps(state, weights[places[rows, i]])
        sorted_rows[at_one, :] = one.astype(F32)
        sorted_rows[at_two, :] = two.astype(F32)
        return carry

    lax.fori_loop(0, places[rows + 8, 0], tile, 0)

    def gather(r, carry):
        for j in range(LANES // GROUP):
            group = places.at[r, pl.ds(j * GROUP, GROUP)]
            for k in range(GROUP):
                at = (r * LANES + j * GROUP + k) * 2
                out[rows2(at), :] = sorted_rows[rows2(group[steps[k]]), :]
        return carry

    lax.fori_loop(0, rows, gather, 0)
    out_copy = pltpu.make_async_copy(out, out_any, sem)
    out_copy.start()
    for k, block in enumerate((out_up, out_down, out_left, out_right)):
        send_rows(exp_s, k * export_lines, steps, out, block, (stage_a, stage_b))
    out_copy.wait()


def vmem():
    return pl.BlockSpec(memory_space=pltpu.VMEM)


def smem():
    return pl.BlockSpec(memory_space=pltpu.SMEM)


def hbm():
    return pl.BlockSpec(memory_space=pltpu.HBM)


def own_cells(dust, classes, kernels, export_ids):
    cells = dust.shape[0]
    export = export_ids.shape[2]
    rows = cells // LANES
    class_count = kernels.shape[0]
    most = cells // TILE + class_count
    block = jax.ShapeDtypeStruct((export, 2 * LANES), BF16)
    return pl.pallas_call(
        functools.partial(own_kernel, cells),
        out_shape=(jax.ShapeDtypeStruct((2 * cells, LANES), F32), block, block, block, block),
        in_specs=[vmem(), vmem(), hbm(), hbm()],
        out_specs=(hbm(), vmem(), vmem(), vmem(), vmem()),
        scratch_shapes=[
            pltpu.VMEM((2 * cells, LANES), F32),
            pltpu.VMEM((cells, 2 * LANES), BF16),
            pltpu.VMEM(kernels.shape, BF16),
            pltpu.VMEM((2 * most * TILE, LANES), F32),
            pltpu.VMEM((class_count, 2 * LANES, 2 * LANES), BF16),
            pltpu.VMEM((rows + 16, LANES), I32),
            pltpu.SMEM((rows + 16, LANES), I32),
            pltpu.VMEM((4 * export // LANES, LANES), I32),
            pltpu.SMEM((4 * export // LANES, LANES), I32),
            pltpu.VMEM((2 * LANES, LANES), F32),
            pltpu.VMEM((2 * LANES, LANES), F32),
            pltpu.SemaphoreType.DMA,
            pltpu.SemaphoreType.DMA((4,)),
            pltpu.SemaphoreType.DMA,
            pltpu.SemaphoreType.DMA,
        ],
        compiler_params=pltpu.CompilerParams(vmem_limit_bytes=VMEM_MIB * MIB),
        cost_estimate=pl.CostEstimate(flops=9_000_000_000, bytes_accessed=12 * MIB, transcendentals=0),
        name="coagulate_own",
    )(classes.reshape(rows, LANES), export_ids, dust, kernels)


def pairs(start):
    return pl.ds(pl.multiple_of(start, 8), CHUNK, stride=2), pl.ds(start + 1, CHUNK, stride=2)


def face_sums(own_one, own_two, weights, stage, face_count):
    one, two = own_one, own_two
    for f in range(face_count):
        c = jnp.broadcast_to(weights[:, f:f + 1], (CHUNK, LANES))
        one = one + c * (stage[pl.ds(2 * f * CHUNK, CHUNK, stride=2), :] - own_one)
        two = two + c * (stage[pl.ds(2 * f * CHUNK + 1, CHUNK, stride=2), :] - own_two)
    return one, two


def turn_columns(coef, coef8, columns):
    together = 4
    coef8[0:coef.shape[0], :] = coef[...]

    def turn(b, carry):
        for u in range(together):
            at = pl.ds(pl.multiple_of((b * together + u) * LANES, LANES), LANES)
            columns[at, :] = coef8[:, at].T
        return carry

    lax.fori_loop(0, columns.shape[0] // (LANES * together), turn, 0)


def start_faces(faces, faces_v, faces_s, sem):
    lines_of(faces, faces_v, 2)
    copy = pltpu.make_async_copy(faces_v, faces_s, sem)
    copy.start()
    return copy


def start_ghosts(ghosts, landed, sems):
    copies = []
    for k, ghost in enumerate(ghosts):
        copies.append(pltpu.make_async_copy(ghost, landed.at[k], sems.at[k]))
        copies[-1].start()
    return copies


def spread_ghosts(copies, landed, table, first):
    for k, copy in enumerate(copies):
        copy.wait()
        spread_rows(landed.at[k], table, first + k * landed.shape[1], landed.shape[1])


def early_kernel(face_count, cells, late_rows, faces, own, coef, out_any, out, table, stage_a, stage_b, coef8, columns,
                 faces_v, faces_s, sem, face_sem, out_sems):
    copy = pltpu.make_async_copy(own, table.at[pl.ds(0, 2 * cells)], sem)
    copy.start()
    face_copy = start_faces(faces, faces_v, faces_s, face_sem)

    def clear(i, carry):
        table[pl.ds(pl.multiple_of(2 * cells + i * 256, 256), 256), :] = jnp.zeros((256, LANES), F32)
        return carry

    lax.fori_loop(0, 2 * late_rows // 256, clear, 0)
    turn_columns(coef, coef8, columns)
    face_copy.wait()
    flat = faces_s.reshape(face_count * cells)
    steps = small_numbers(faces_s[0, 0])
    copy.wait()

    def pull(i, stage):
        for f in range(face_count):
            for j in range(CHUNK // GROUP):
                group = flat.at[pl.ds(i * CHUNK + (f * cells + j * GROUP), GROUP)]
                for k in range(GROUP):
                    stage[rows2((f * CHUNK + j * GROUP + k) * 2), :] = table[rows2(group[steps[k]]), :]

    def push(i, stage):
        at = pairs(i * (2 * CHUNK))
        weights = columns[pl.ds(pl.multiple_of(i * CHUNK, CHUNK), CHUNK), :]
        one, two = face_sums(table[at[0], :], table[at[1], :], weights, stage, face_count)
        out[at[0], :] = one
        out[at[1], :] = two

    pull(0, stage_a)
    chunks = cells // CHUNK

    def pair(i, carry):
        push(2 * i, stage_a)
        pull(2 * i + 1, stage_b)
        push(2 * i + 1, stage_b)
        pull(jnp.minimum(2 * i + 2, chunks - 1), stage_a)
        return carry

    parts = out_sems.shape[0]
    done = []
    for p in range(parts):
        lax.fori_loop(p * (chunks // 2 // parts), (p + 1) * (chunks // 2 // parts), pair, 0)
        at = pl.ds(p * (2 * cells // parts), 2 * cells // parts)
        done.append(pltpu.make_async_copy(out.at[at], out_any.at[at], out_sems.at[p]))
        done[-1].start()
    for part in done:
        part.wait()


def diffuse_early(faces, own, coef, late_rows):
    face_count, cells = coef.shape
    padded = face_count + -face_count % 8
    return pl.pallas_call(
        functools.partial(early_kernel, face_count, cells, late_rows),
        out_shape=jax.ShapeDtypeStruct((2 * cells, LANES), F32),
        in_specs=[vmem(), hbm(), vmem()],
        out_specs=hbm(),
        scratch_shapes=[
            pltpu.VMEM((2 * cells, LANES), F32),
            pltpu.VMEM((2 * (cells + late_rows), LANES), F32),
            pltpu.VMEM((2 * face_count * CHUNK, LANES), F32),
            pltpu.VMEM((2 * face_count * CHUNK, LANES), F32),
            pltpu.VMEM((padded, cells), F32),
            pltpu.VMEM((cells, padded), F32),
            pltpu.VMEM((face_count * cells // LANES, LANES), I32),
            pltpu.SMEM((face_count * cells // LANES, LANES), I32),
            pltpu.SemaphoreType.DMA,
            pltpu.SemaphoreType.DMA,
            pltpu.SemaphoreType.DMA((4,)),
        ],
        compiler_params=pltpu.CompilerParams(vmem_limit_bytes=VMEM_MIB * MIB),
        cost_estimate=pl.CostEstimate(flops=20_000_000_000, bytes_accessed=16 * MIB, transcendentals=0),
        name="diffuse_early",
    )(faces, own, coef)


def leave_kernel(face_count, cells, faces, mig, counts, own, g0, g1, g2, g3, coef, out, table, landed, stage, own_stage, coef8,
                 columns, coef_stage, faces_v, faces_s, sem, face_sem, ghost_sems):
    ghost_copies = start_ghosts((g0, g1, g2, g3), landed, ghost_sems)
    copy = pltpu.make_async_copy(own, table.at[pl.ds(0, 2 * cells)], sem)
    copy.start()
    face_copy = start_faces(faces, faces_v, faces_s, face_sem)
    turn_columns(coef, coef8, columns)
    spread_ghosts(ghost_copies, landed, table, cells)
    face_copy.wait()
    flat = faces_s.reshape(face_count * cells)
    copy.wait()

    def chunk(i, carry):
        for u in range(CHUNK):
            cell = mig[i, u]
            own_stage[rows2(2 * u), :] = table[rows2(2 * cell), :]
            coef_stage[pl.ds(u, 1), :] = columns[pl.ds(cell, 1), :]
            for f in range(face_count):
                stage[rows2((f * CHUNK + u) * 2), :] = table[rows2(flat.at[pl.ds(f * cells, cells)][cell]), :]
        one, two = face_sums(own_stage[pl.ds(0, CHUNK, stride=2), :], own_stage[pl.ds(1, CHUNK, stride=2), :],
                             coef_stage[...], stage, face_count)
        at = pl.ds(pl.multiple_of(i * CHUNK, CHUNK), CHUNK)
        keep = iota2((CHUNK, LANES), 0) < counts[0, i]
        out[at, 0:LANES] = jnp.where(keep, one, 0.0).astype(BF16)
        out[at, LANES:2 * LANES] = jnp.where(keep, two, 0.0).astype(BF16)
        return carry

    lax.fori_loop(0, out.shape[0] // CHUNK, chunk, 0)


def diffuse_leaving(faces, mig, counts, own, ghosts, coef):
    face_count, cells = coef.shape
    padded = face_count + -face_count % 8
    ghost_rows = sum(g.shape[0] for g in ghosts)
    return pl.pallas_call(
        functools.partial(leave_kernel, face_count, cells),
        out_shape=jax.ShapeDtypeStruct((mig.shape[0] * CHUNK, 2 * LANES), BF16),
        in_specs=[vmem(), smem(), smem()] + [hbm()] * 5 + [vmem()],
        out_specs=vmem(),
        scratch_shapes=[
            pltpu.VMEM((2 * (cells + ghost_rows), LANES), F32),
            pltpu.VMEM((len(ghosts),) + ghosts[0].shape, BF16),
            pltpu.VMEM((2 * face_count * CHUNK, LANES), F32),
            pltpu.VMEM((2 * CHUNK, LANES), F32),
            pltpu.VMEM((padded, cells), F32),
            pltpu.VMEM((cells, padded), F32),
            pltpu.VMEM((CHUNK, padded), F32),
            pltpu.VMEM((face_count * cells // LANES, LANES), I32),
            pltpu.SMEM((face_count * cells // LANES, LANES), I32),
            pltpu.SemaphoreType.DMA,
            pltpu.SemaphoreType.DMA,
            pltpu.SemaphoreType.DMA((len(ghosts),)),
        ],
        compiler_params=pltpu.CompilerParams(vmem_limit_bytes=VMEM_MIB * MIB),
        cost_estimate=pl.CostEstimate(flops=500_000_000, bytes_accessed=8 * MIB, transcendentals=0),
        name="diffuse_leaving",
    )(faces, mig, counts, own, *ghosts, coef)


def list_kernel(face_count, cells, shift, faces, out, turned):
    rows = cells // LANES
    place = iota2((rows, LANES), 0) * LANES + iota2((rows, LANES), 1)
    words = []
    lines_of(faces, turned, 2)
    for f in range(face_count):
        to = turned[f * rows:(f + 1) * rows, :]
        late = to >= 2 * cells
        number = jnp.sum(late.astype(F32), keepdims=True).astype(I32)
        out[face_count * rows + f:face_count * rows + f + 1, :] = jnp.broadcast_to(number, (1, LANES))
        words.append(jnp.where(late, ((2 * place) << shift) + (to - 2 * cells), (2 * cells) << shift))
    size = 2
    while size <= cells:
        apart = size // 2
        while apart >= 1:
            low = (place & apart) == 0
            smaller = (((place >> (size.bit_length() - 1)) ^ (place >> (apart.bit_length() - 1))) & 1) == 0
            for f in range(face_count):
                x = words[f]
                axis, by, length = (1, apart, LANES) if apart < LANES else (0, apart // LANES, rows)
                other = jnp.where(low, pltpu.roll(x, length - by, axis), pltpu.roll(x, by, axis))
                words[f] = jnp.where(smaller, jnp.minimum(x, other), jnp.maximum(x, other))
            apart //= 2
        size *= 2
    for f in range(face_count):
        out[f * rows:(f + 1) * rows, :] = words[f]


def late_lists(faces, shift, after):
    face_count, cells = faces.shape
    rows = face_count * cells // LANES
    return pl.pallas_call(
        lambda faces, after_ref, out, turned: list_kernel(face_count, cells, shift, faces, out, turned),
        out_shape=jax.ShapeDtypeStruct((rows + 8, LANES), I32),
        in_specs=[vmem(), hbm()],
        out_specs=vmem(),
        scratch_shapes=[pltpu.VMEM((rows, LANES), I32)],
        compiler_params=pltpu.CompilerParams(vmem_limit_bytes=VMEM_MIB * MIB),
        cost_estimate=pl.CostEstimate(flops=2_000_000_000, bytes_accessed=1 * MIB, transcendentals=0),
        name="late_lists",
    )(faces, after)


def late_kernel(face_count, cells, shift, lists, coef, early, g0, g1, g2, g3, out, sums, table, landed, coef_v, coef_s, sem,
                ghost_sems, coef_sem):
    ghost_copies = start_ghosts((g0, g1, g2, g3), landed, ghost_sems)
    copy = pltpu.make_async_copy(early, sums.at[pl.ds(0, 2 * cells)], sem)
    copy.start()
    lines_of(coef, coef_v, 1.0)
    coef_copy = pltpu.make_async_copy(coef_v, coef_s, coef_sem)
    coef_copy.start()
    spread_ghosts(ghost_copies, landed, table, 0)
    steps = small_numbers(lists[0])
    coef_copy.wait()
    flat = coef_s.reshape(face_count * cells)
    copy.wait()
    for f in range(face_count):
        def some(i, carry):
            found = []
            for j in range(CHUNK // GROUP):
                group = lists.at[pl.ds(i * CHUNK + (f * cells + j * GROUP), GROUP)]
                for k in range(GROUP):
                    word = group[steps[k]]
                    row = rows2(word >> shift)
                    weight = flat.at[pl.ds(f * cells, cells)][jnp.minimum(word >> (shift + 1), cells - 1)]
                    late = table[rows2(word & ((1 << shift) - 1)), :]
                    found.append((row, sums[row, :] + weight * late))
            for row, value in found:
                sums[row, :] = value
            return carry

        lax.fori_loop(0, (lists[face_count * cells + f * LANES] + (CHUNK - 1)) // CHUNK, some, 0)
    span = 256

    def pack(i, carry):
        at = pl.ds(pl.multiple_of(i * span, span), span)
        out[at, 0:LANES] = sums[pl.ds(pl.multiple_of(i * 2 * span, span), span, stride=2), :].astype(BF16)
        out[at, LANES:2 * LANES] = sums[pl.ds(i * 2 * span + 1, span, stride=2), :].astype(BF16)
        return carry

    lax.fori_loop(0, cells // span, pack, 0)


def diffuse_late(lists, coef, early, ghosts, shift):
    face_count, cells = coef.shape
    ghost_rows = sum(g.shape[0] for g in ghosts)
    return pl.pallas_call(
        functools.partial(late_kernel, face_count, cells, shift),
        out_shape=jax.ShapeDtypeStruct((cells, 2 * LANES), BF16),
        in_specs=[smem(), vmem(), hbm()] + [hbm()] * len(ghosts),
        out_specs=vmem(),
        scratch_shapes=[
            pltpu.VMEM((2 * cells + 16, LANES), F32),
            pltpu.VMEM((2 * ghost_rows, LANES), F32),
            pltpu.VMEM((len(ghosts),) + ghosts[0].shape, BF16),
            pltpu.VMEM((face_count * cells // LANES, LANES), F32),
            pltpu.SMEM((face_count * cells // LANES, LANES), F32),
            pltpu.SemaphoreType.DMA,
            pltpu.SemaphoreType.DMA((len(ghosts),)),
            pltpu.SemaphoreType.DMA,
        ],
        compiler_params=pltpu.CompilerParams(vmem_limit_bytes=VMEM_MIB * MIB),
        cost_estimate=pl.CostEstimate(flops=9_000_000_000, bytes_accessed=24 * MIB, transcendentals=0),
        name="diffuse_late",
    )(lists, coef, early, *ghosts)


def body(dust, classes, kernels, export_ids, faces, face_coef, mig_ids, mig_counts):
    row_width = dust.shape[1]
    export = export_ids.shape[2]
    domains = mig_counts.shape[1]
    capacity = mig_ids.shape[1]
    shift = (8 * export - 1).bit_length()
    own, up, down, left, right = own_cells(dust, classes, kernels, export_ids)
    g0, g1 = passed_along(up, "dx", 1), passed_along(down, "dx", -1)
    g2, g3 = passed_along(left, "dy", 1), passed_along(right, "dy", -1)
    ghosts = (g0, g1, g2, g3)
    faces, face_coef, mig_ids, own = lax.optimization_barrier((faces, face_coef, mig_ids, own))
    early = diffuse_early(faces, own, face_coef, 4 * export)
    lists = late_lists(faces, shift, own)
    leaving = diffuse_leaving(faces, mig_ids, mig_counts, own, ghosts, face_coef)
    arrived = lax.all_to_all(leaving.reshape(domains, capacity, row_width), ("dx", "dy"), split_axis=0, concat_axis=0, tiled=True)
    updated = diffuse_late(lists.reshape(-1), face_coef, early, ghosts, shift)
    return (updated, arrived.reshape(domains * capacity, row_width))


def solution(mesh):
    return jax.shard_map(
        body,
        mesh=mesh,
        in_specs=(
            P(("dx", "dy"), None),
            P(("dx", "dy")),
            P(),
            P(("dx", "dy"), None, None),
            P(None, ("dx", "dy")),
            P(None, ("dx", "dy")),
            P(("dx", "dy"), None),
            P(("dx", "dy"), None),
        ),
        out_specs=(P(("dx", "dy"), None), P(("dx", "dy"), None)),
        check_vma=False,
    )
```

```python
import functools

import jax
import jax.numpy as jnp
from jax import lax
from jax.experimental import pallas as pl
from jax.experimental.pallas import tpu as pltpu
from jax.sharding import PartitionSpec as P

SUBSTEPS = 6
LANES = 128
GROUP = 8
TILE = 576
CHUNK = 16
BATCH = 32
FIRST_LINES = 16
F32 = jnp.float32
BF16 = jnp.bfloat16
I32 = jnp.int32
KIB = 1 << 10
MIB = 1 << 20
VMEM_KIB = 65330
LESS_VMEM_KIB = 61440


def passed_along(block, axis, distance):
    devices = range(lax.axis_size(axis))
    route = [((i - distance) % len(devices), i) for i in devices]
    return lax.ppermute(block, axis, route)


def iota2(shape, dim):
    return lax.broadcasted_iota(I32, shape, dim)


def small_numbers(none_negative, count=GROUP, apart=1):
    unit = jnp.minimum(none_negative, 0) + apart
    return [unit * k for k in range(count)]


def lines_of(source, lines, times):
    per_row = source.shape[1] // LANES
    for r in range(source.shape[0]):
        for i in range(per_row):
            at = r * per_row + i
            lines[at:at + 1, :] = source[r:r + 1, i * LANES:(i + 1) * LANES] * times


def dot(a, b):
    return jnp.dot(a, b, preferred_element_type=F32)


def rows2(start):
    return pl.ds(pl.multiple_of(start, 2), 2)


def spread_rows(src, table, first, count):
    step = 256

    def one(i, carry):
        block = src[pl.ds(pl.multiple_of(i * step, step), step), :].astype(F32)
        at = 2 * first + i * (2 * step)
        table[pl.ds(pl.multiple_of(at, 8), step, stride=2), :] = block[:, :LANES]
        table[pl.ds(at + 1, step, stride=2), :] = block[:, LANES:]
        return carry

    lax.fori_loop(0, count // step, one, 0)


def class_places(cls, class_count, tile):
    rows = cls.shape[0]
    shift = rows.bit_length() - 1
    wide = class_count * rows
    member = jnp.concatenate([(cls == c).astype(F32) for c in range(class_count)], axis=0)
    member16 = member.astype(BF16)
    before = (iota2((LANES, LANES), 0) < iota2((LANES, LANES), 1)).astype(F32).astype(BF16)
    in_row = dot(member16, before)
    row_total = dot(member16, jnp.ones((LANES, LANES), BF16)).astype(BF16)
    a, b = iota2((wide, wide), 0), iota2((wide, wide), 1)
    same = (a >> shift) == (b >> shift)
    earlier_rows = jnp.logical_and(same, b < a).astype(F32).astype(BF16)
    row_start = dot(earlier_rows, row_total)
    class_total = dot(same.astype(F32).astype(BF16), row_total)
    tiles = ((class_total + (tile - 0.5)) * (1.0 / tile)).astype(I32).astype(F32)
    earlier = jnp.logical_and((b >> shift) < (a >> shift), (b & (rows - 1)) == 0)
    first_tile = dot(earlier.astype(F32).astype(BF16), tiles.astype(BF16))
    place = member * (first_tile * float(tile) + row_start + in_row)
    total = place[:rows]
    for c in range(1, class_count):
        total = total + place[c * rows:(c + 1) * rows]
    last_tile = (first_tile + tiles).astype(I32)
    lane = iota2((8, LANES), 1)
    tile_class = jnp.zeros((8, LANES), I32)
    for c in range(class_count - 1):
        tile_class = tile_class + (last_tile[c * rows:c * rows + 8] <= lane).astype(I32)
    tile_count = last_tile[wide - 8:]
    return (2.0 * total).astype(I32), tile_class, tile_count


def substeps(state, weights):
    one, two = state[:, :LANES], state[:, LANES:]
    bins = float(LANES)
    for _ in range(SUBSTEPS):
        operand = jnp.concatenate([one, two], axis=1).astype(BF16)
        square_one = jnp.sum(one * one, axis=1, keepdims=True)
        square_two = jnp.sum(two * two, axis=1, keepdims=True)
        product = dot(operand, weights)
        one = one + product[:, :LANES] * (1.0 / bins - pl.reciprocal(bins + square_one, approx=True))
        two = two + product[:, LANES:] * (1.0 / bins - pl.reciprocal(bins + square_two, approx=True))
    return one.astype(BF16), two.astype(BF16)


def send_rows(ids, steps, table, outbound, stages):
    span = LANES
    lines = ids.shape[0]

    def pull(line, stage):
        for j in range(span // GROUP):
            group = ids.at[line, pl.ds(j * GROUP, GROUP)]
            for k in range(GROUP):
                stage[rows2((j * GROUP + k) * 2), :] = table[rows2(group[steps[k]]), :]

    def push(block, i, stage):
        at = pl.ds(pl.multiple_of(i * span, span), span)
        block[at, 0:LANES] = stage[pl.ds(0, span, stride=2), :].astype(BF16)
        block[at, LANES:2 * LANES] = stage[pl.ds(1, span, stride=2), :].astype(BF16)

    pull(0, stages[0])
    first = 0
    for block in outbound:
        spans = block.shape[0] // span

        def pair(i, carry):
            push(block, 2 * i, stages[0])
            pull(first + 2 * i + 1, stages[1])
            push(block, 2 * i + 1, stages[1])
            pull(jnp.minimum(first + 2 * i + 2, lines - 1), stages[0])
            return carry

        lax.fori_loop(0, spans // 2, pair, 0)
        first += spans


def own_kernel(cells, cls_ref, exp_ref, dust_any, kern_any, out_any, out_up, out_down, out_left, out_right,
               out, dust, kern, sorted_rows, weights, places_v, places, exp_v, exp_s, stage_a, stage_b, sem, dust_sems, kern_sem, exp_sem):
    class_count = kern.shape[0]
    rows = cells // LANES
    parts = dust_sems.shape[0]
    part = cells // parts
    kern_copy = pltpu.make_async_copy(kern_any, kern, kern_sem)
    kern_copy.start()
    dust_copies = []
    for p in range(parts):
        at = pl.ds(p * part, part)
        dust_copies.append(pltpu.make_async_copy(dust_any.at[at], dust.at[at], dust_sems.at[p]))
        dust_copies[-1].start()
    lines_of(exp_ref.at[0], exp_v, 2)
    exp_copy = pltpu.make_async_copy(exp_v, exp_s, exp_sem)
    exp_copy.start()
    place, tile_class, tile_count = class_places(cls_ref[...], class_count, TILE)
    places_v[0:rows, :] = place
    places_v[rows:rows + 8, :] = tile_class
    places_v[rows + 8:rows + 16, :] = tile_count
    copy = pltpu.make_async_copy(places_v, places, sem)
    copy.start()
    zero = jnp.zeros((LANES, LANES), BF16)
    kern_copy.wait()
    for c in range(class_count):
        for s in range(2):
            own = kern[c, s].astype(F32) * float(LANES)
            weights[c, s * LANES:(s + 1) * LANES, s * LANES:(s + 1) * LANES] = own.astype(BF16)
            weights[c, s * LANES:(s + 1) * LANES, (1 - s) * LANES:(2 - s) * LANES] = zero
    for dust_copy in dust_copies:
        dust_copy.wait()
    copy.wait()
    exp_copy.wait()
    steps = small_numbers(places[0, 0])

    def widen(r, stage):
        block = dust[pl.ds(pl.multiple_of(r * LANES, LANES), LANES), :].astype(F32)
        stage[pl.ds(0, LANES, stride=2), :] = block[:, :LANES]
        stage[pl.ds(1, LANES, stride=2), :] = block[:, LANES:]

    def scatter(r, stage):
        for j in range(LANES // GROUP):
            group = places.at[r, pl.ds(j * GROUP, GROUP)]
            for k in range(GROUP):
                sorted_rows[rows2(group[steps[k]]), :] = stage[rows2((j * GROUP + k) * 2), :]

    widen(0, stage_a)

    def pair(i, carry):
        scatter(2 * i, stage_a)
        widen(2 * i + 1, stage_b)
        scatter(2 * i + 1, stage_b)
        widen(jnp.minimum(2 * i + 2, rows - 1), stage_a)
        return carry

    lax.fori_loop(0, rows // 2, pair, 0)

    def tile(i, carry):
        first = i * (2 * TILE)
        at_one = pl.ds(pl.multiple_of(first, 8), TILE, stride=2)
        at_two = pl.ds(first + 1, TILE, stride=2)
        state = jnp.concatenate([sorted_rows[at_one, :], sorted_rows[at_two, :]], axis=1)
        one, two = substeps(state, weights[places[rows, i]])
        sorted_rows[at_one, :] = one.astype(F32)
        sorted_rows[at_two, :] = two.astype(F32)
        return carry

    lax.fori_loop(0, places[rows + 8, 0], tile, 0)

    def gather(r, carry):
        for j in range(LANES // GROUP):
            group = places.at[r, pl.ds(j * GROUP, GROUP)]
            for k in range(GROUP):
                at = (r * LANES + j * GROUP + k) * 2
                out[rows2(at), :] = sorted_rows[rows2(group[steps[k]]), :]
        return carry

    lax.fori_loop(0, rows, gather, 0)
    out_copy = pltpu.make_async_copy(out, out_any, sem)
    out_copy.start()
    send_rows(exp_s, steps, out, (out_up, out_down, out_left, out_right), (stage_a, stage_b))
    out_copy.wait()


def vmem():
    return pl.BlockSpec(memory_space=pltpu.VMEM)


def smem():
    return pl.BlockSpec(memory_space=pltpu.SMEM)


def anywhere():
    return pl.BlockSpec(memory_space=pl.ANY)


def hbm():
    return pl.BlockSpec(memory_space=pltpu.HBM)


def own_cells(dust, classes, kernels, export_ids):
    cells = dust.shape[0]
    export = export_ids.shape[2]
    rows = cells // LANES
    class_count = kernels.shape[0]
    most = cells // TILE + class_count
    block = jax.ShapeDtypeStruct((export, 2 * LANES), BF16)
    return pl.pallas_call(
        functools.partial(own_kernel, cells),
        out_shape=(jax.ShapeDtypeStruct((2 * cells, LANES), F32), block, block, block, block),
        in_specs=[vmem(), vmem(), hbm(), hbm()],
        out_specs=(hbm(), vmem(), vmem(), vmem(), vmem()),
        scratch_shapes=[
            pltpu.VMEM((2 * cells, LANES), F32),
            pltpu.VMEM((cells, 2 * LANES), BF16),
            pltpu.VMEM(kernels.shape, BF16),
            pltpu.VMEM((2 * most * TILE, LANES), F32),
            pltpu.VMEM((class_count, 2 * LANES, 2 * LANES), BF16),
            pltpu.VMEM((rows + 16, LANES), I32),
            pltpu.SMEM((rows + 16, LANES), I32),
            pltpu.VMEM((4 * export // LANES, LANES), I32),
            pltpu.SMEM((4 * export // LANES, LANES), I32),
            pltpu.VMEM((2 * LANES, LANES), F32),
            pltpu.VMEM((2 * LANES, LANES), F32),
            pltpu.SemaphoreType.DMA,
            pltpu.SemaphoreType.DMA((4,)),
            pltpu.SemaphoreType.DMA,
            pltpu.SemaphoreType.DMA,
        ],
        compiler_params=pltpu.CompilerParams(vmem_limit_bytes=VMEM_KIB * KIB),
        cost_estimate=pl.CostEstimate(flops=9_000_000_000, bytes_accessed=12 * MIB, transcendentals=0),
        name="coagulate_own",
    )(classes.reshape(rows, LANES), export_ids, dust, kernels)


def pairs(start):
    return pl.ds(pl.multiple_of(start, 8), CHUNK, stride=2), pl.ds(start + 1, CHUNK, stride=2)


def face_sums(own_one, own_two, weights, stage, face_count):
    one, two = own_one, own_two
    for f in range(face_count):
        c = jnp.broadcast_to(weights[:, f:f + 1], (CHUNK, LANES))
        one = one + c * (stage[pl.ds(2 * f * CHUNK, CHUNK, stride=2), :] - own_one)
        two = two + c * (stage[pl.ds(2 * f * CHUNK + 1, CHUNK, stride=2), :] - own_two)
    return one, two


def turn_columns(coef, coef8, columns):
    together = 4
    if coef is not None:
        coef8[0:coef.shape[0], :] = coef[...]

    def turn(b, carry):
        for u in range(together):
            at = pl.ds(pl.multiple_of((b * together + u) * LANES, LANES), LANES)
            columns[at, :] = coef8[:, at].T
        return carry

    lax.fori_loop(0, columns.shape[0] // (LANES * together), turn, 0)


def start_faces(faces, faces_v, faces_s, sem):
    lines_of(faces, faces_v, 2)
    copy = pltpu.make_async_copy(faces_v, faces_s, sem)
    copy.start()
    return copy


def start_ghosts(ghosts, landed, sems):
    copies = []
    for k, ghost in enumerate(ghosts):
        copies.append(pltpu.make_async_copy(ghost, landed.at[k], sems.at[k]))
        copies[-1].start()
    return copies


def spread_ghosts(copies, landed, table, first):
    for k, copy in enumerate(copies):
        copy.wait()
        spread_rows(landed.at[k], table, first + k * landed.shape[1], landed.shape[1])


def late_lists(face_count, cells, shift, out, counts, lines):
    per_face = cells // LANES
    blocks = per_face // 8
    lane, sub = iota2((8, LANES), 1), iota2((8, LANES), 0)
    words = []
    for f in range(face_count):
        number = None
        words.append([])
        for v in range(blocks):
            first = f * per_face + v * 8
            to = lines[first:first + 8, :]
            late = to >= 2 * cells
            cell = (sub + v * 8) * LANES + lane
            words[f].append(jnp.where(late, (cell << shift) + (to - 2 * cells), cells << shift))
            counted = late.astype(F32)
            number = counted if number is None else number + counted
        number = jnp.sum(number, keepdims=True).astype(I32)
        counts[f:f + 1, :] = jnp.broadcast_to(number, (1, LANES))
    block_bits = blocks.bit_length() - 1

    def bit(b, v):
        if b < block_bits:
            return bool((v >> b) & 1)
        if b < block_bits + 3:
            return ((sub >> (b - block_bits)) & 1) == 1
        if b < block_bits + 3 + 7:
            return ((lane >> (b - block_bits - 3)) & 1) == 1
        return False

    def pick(where_true, a, b):
        if isinstance(where_true, bool):
            return a if where_true else b
        return jnp.where(where_true, a, b)

    def same(a, b):
        if isinstance(a, bool) and isinstance(b, bool):
            return a == b
        if isinstance(a, bool):
            a, b = b, a
        if isinstance(b, bool):
            return a if b else jnp.logical_not(a)
        return jnp.logical_not(jnp.logical_xor(a, b))

    bits = cells.bit_length() - 1
    for size_bit in range(1, bits + 1):
        for b in range(size_bit - 1, -1, -1):
            for v in range(blocks):
                if b < block_bits and bit(b, v):
                    continue
                down = bit(size_bit, v)
                if b >= block_bits:
                    high = bit(b, v)
                    largest = jnp.logical_not(same(high, down)) if not isinstance(down, bool) else same(high, not down)
                for f in range(face_count):
                    x = words[f][v]
                    if b < block_bits:
                        w = v ^ (1 << b)
                        y = words[f][w]
                        least, most = jnp.minimum(x, y), jnp.maximum(x, y)
                        words[f][v] = pick(down, most, least)
                        words[f][w] = pick(down, least, most)
                        continue
                    axis, by, length = (0, 1 << (b - block_bits), 8)
                    if b >= block_bits + 3:
                        axis, by, length = (1, 1 << (b - block_bits - 3), LANES)
                    other = pltpu.roll(x, by, axis)
                    if 2 * by < length:
                        other = jnp.where(high, other, pltpu.roll(x, length - by, axis))
                    words[f][v] = pick(largest, jnp.maximum(x, other), jnp.minimum(x, other))
    for f in range(face_count):
        word = jnp.concatenate(words[f], axis=0)
        both = jnp.concatenate([word >> shift, word & ((1 << shift) - 1)], axis=0)
        out[f * LANES:(f + 1) * LANES, 0:2 * per_face] = both.T


def early_kernel(face_count, cells, late_rows, shift, faces, mig, own, coef, out_any, mig_sums, mig_coef, mig_late, lists, counts,
                 out, table,
                 stage_a, stage_b, coef8, columns, late8, late_columns, mig_columns, faces_v, faces_s, sem, face_sem, out_sems):
    copy = pltpu.make_async_copy(own, table.at[pl.ds(0, 2 * cells)], sem)
    copy.start()
    face_copy = start_faces(faces, faces_v, faces_s, face_sem)

    def clear(i, carry):
        table[pl.ds(pl.multiple_of(2 * cells + i * 256, 256), 256), :] = jnp.zeros((256, LANES), F32)
        return carry

    lax.fori_loop(0, 2 * late_rows // 256, clear, 0)
    turn_columns(coef, coef8, columns)
    late8[0:face_count, :] = jnp.where(faces[...] >= cells, 2 * (faces[...] - cells), 2 * late_rows)
    turn_columns(None, late8, late_columns)
    late_lists(face_count, cells, shift, lists, counts, faces_v)
    face_copy.wait()
    flat = faces_s.reshape(face_count * cells)
    steps = small_numbers(faces_s[0, 0])
    copy.wait()

    def pull(i, stage):
        for f in range(face_count):
            for j in range(CHUNK // GROUP):
                group = flat.at[pl.ds(i * CHUNK + (f * cells + j * GROUP), GROUP)]
                for k in range(GROUP):
                    stage[rows2((f * CHUNK + j * GROUP + k) * 2), :] = table[rows2(group[steps[k]]), :]

    def push(i, stage):
        at = pairs(i * (2 * CHUNK))
        weights = columns[pl.ds(pl.multiple_of(i * CHUNK, CHUNK), CHUNK), :]
        one, two = face_sums(table[at[0], :], table[at[1], :], weights, stage, face_count)
        out[at[0], :] = one
        out[at[1], :] = two

    pull(0, stage_a)
    chunks = cells // CHUNK

    def pair(i, carry):
        push(2 * i, stage_a)
        pull(2 * i + 1, stage_b)
        push(2 * i + 1, stage_b)
        pull(jnp.minimum(2 * i + 2, chunks - 1), stage_a)
        return carry

    parts = out_sems.shape[0]
    done = []
    for p in range(parts):
        lax.fori_loop(p * (chunks // 2 // parts), (p + 1) * (chunks // 2 // parts), pair, 0)
        at = pl.ds(p * (2 * cells // parts), 2 * cells // parts)
        done.append(pltpu.make_async_copy(out.at[at], out_any.at[at], out_sems.at[p]))
        done[-1].start()

    def leaving(i, carry):
        for u in range(CHUNK):
            cell = mig[u, i]
            at = i * CHUNK + u
            mig_sums[rows2(2 * at), :] = out[rows2(2 * cell), :]
            mig_coef[pl.ds(at, 1), :] = columns[pl.ds(cell, 1), :]
            mig_columns[pl.ds(at, 1), :] = late_columns[pl.ds(cell, 1), :]
        return carry

    lax.fori_loop(0, mig.shape[1], leaving, 0)
    lines = mig_columns.shape[0] // LANES
    for i in range(lines):
        turned = mig_columns[i * LANES:(i + 1) * LANES, :].T
        for f in range(face_count):
            mig_late[f * lines + i:f * lines + i + 1, :] = turned[f:f + 1, :]
    for part in done:
        part.wait()


def diffuse_early(faces, mig, own, coef, late_rows, shift):
    face_count, cells = coef.shape
    padded = face_count + -face_count % 8
    leaving = mig.shape[0] * mig.shape[1]
    return pl.pallas_call(
        functools.partial(early_kernel, face_count, cells, late_rows, shift),
        out_shape=(
            jax.ShapeDtypeStruct((2 * cells, LANES), F32),
            jax.ShapeDtypeStruct((2 * leaving, LANES), F32),
            jax.ShapeDtypeStruct((leaving, padded), F32),
            jax.ShapeDtypeStruct((face_count * leaving // LANES, LANES), I32),
            jax.ShapeDtypeStruct((face_count * LANES, LANES), I32),
            jax.ShapeDtypeStruct((8, LANES), I32),
        ),
        in_specs=[vmem(), smem(), hbm(), vmem()],
        out_specs=(hbm(), vmem(), vmem(), vmem(), vmem(), vmem()),
        scratch_shapes=[
            pltpu.VMEM((2 * cells, LANES), F32),
            pltpu.VMEM((2 * (cells + late_rows), LANES), F32),
            pltpu.VMEM((2 * face_count * CHUNK, LANES), F32),
            pltpu.VMEM((2 * face_count * CHUNK, LANES), F32),
            pltpu.VMEM((padded, cells), F32),
            pltpu.VMEM((cells, padded), F32),
            pltpu.VMEM((padded, cells), I32),
            pltpu.VMEM((cells, padded), I32),
            pltpu.VMEM((leaving, padded), I32),
            pltpu.VMEM((face_count * cells // LANES, LANES), I32),
            pltpu.SMEM((face_count * cells // LANES, LANES), I32),
            pltpu.SemaphoreType.DMA,
            pltpu.SemaphoreType.DMA,
            pltpu.SemaphoreType.DMA((4,)),
        ],
        compiler_params=pltpu.CompilerParams(vmem_limit_bytes=VMEM_KIB * KIB),
        cost_estimate=pl.CostEstimate(flops=20_000_000_000, bytes_accessed=16 * MIB, transcendentals=0),
        name="diffuse_early",
    )(faces, mig, own, coef)


def leave_kernel(face_count, late_any, counts, sums_any, coef_any, g0, g1, g2, g3, out, table, landed, stage_a, stage_b,
                 late_s, mig_sums, mig_coef, late_sem, sums_sem, coef_sem, ghost_sems):
    ghost_copies = start_ghosts((g0, g1, g2, g3), landed, ghost_sems)
    copies = [
        pltpu.make_async_copy(late_any, late_s, late_sem),
        pltpu.make_async_copy(sums_any, mig_sums, sums_sem),
        pltpu.make_async_copy(coef_any, mig_coef, coef_sem),
    ]
    for copy in copies:
        copy.start()
    ghost_rows = landed.shape[0] * landed.shape[1]
    table[2 * ghost_rows:2 * ghost_rows + 8, :] = jnp.zeros((8, LANES), F32)
    spread_ghosts(ghost_copies, landed, table, 0)
    for copy in copies:
        copy.wait()
    cells = out.shape[0]
    mig_late = late_s.reshape(face_count * cells)
    steps = small_numbers(late_s[0, 0])
    chunks = cells // CHUNK

    def pull(i, stage):
        for f in range(face_count):
            for j in range(CHUNK // GROUP):
                group = mig_late.at[pl.ds(i * CHUNK + (f * cells + j * GROUP), GROUP)]
                for k in range(GROUP):
                    stage[rows2((f * CHUNK + j * GROUP + k) * 2), :] = table[rows2(group[steps[k]]), :]

    def push(i, stage):
        at = pairs(i * (2 * CHUNK))
        here = pl.ds(pl.multiple_of(i * CHUNK, CHUNK), CHUNK)
        one, two = mig_sums[at[0], :], mig_sums[at[1], :]
        weights = mig_coef[here, :]
        for f in range(face_count):
            c = jnp.broadcast_to(weights[:, f:f + 1], (CHUNK, LANES))
            one = one + c * stage[pl.ds(2 * f * CHUNK, CHUNK, stride=2), :]
            two = two + c * stage[pl.ds(2 * f * CHUNK + 1, CHUNK, stride=2), :]
        keep = iota2((CHUNK, LANES), 0) < counts[0, i]
        out[here, 0:LANES] = jnp.where(keep, one, 0.0).astype(BF16)
        out[here, LANES:2 * LANES] = jnp.where(keep, two, 0.0).astype(BF16)

    pull(0, stage_a)

    def pair(i, carry):
        push(2 * i, stage_a)
        pull(2 * i + 1, stage_b)
        push(2 * i + 1, stage_b)
        pull(jnp.minimum(2 * i + 2, chunks - 1), stage_a)
        return carry

    lax.fori_loop(0, chunks // 2, pair, 0)


def diffuse_leaving(mig_late, counts, mig_sums, mig_coef, ghosts, face_count):
    ghost_rows = sum(g.shape[0] for g in ghosts)
    return pl.pallas_call(
        functools.partial(leave_kernel, face_count),
        out_shape=jax.ShapeDtypeStruct((mig_coef.shape[0], 2 * LANES), BF16),
        in_specs=[anywhere(), smem(), anywhere(), anywhere()] + [anywhere()] * 4,
        out_specs=vmem(),
        scratch_shapes=[
            pltpu.VMEM((2 * ghost_rows + 8, LANES), F32),
            pltpu.VMEM((len(ghosts),) + ghosts[0].shape, BF16),
            pltpu.VMEM((2 * face_count * CHUNK, LANES), F32),
            pltpu.VMEM((2 * face_count * CHUNK, LANES), F32),
            pltpu.SMEM(mig_late.shape, I32),
            pltpu.VMEM(mig_sums.shape, F32),
            pltpu.VMEM(mig_coef.shape, F32),
            pltpu.SemaphoreType.DMA,
            pltpu.SemaphoreType.DMA,
            pltpu.SemaphoreType.DMA,
            pltpu.SemaphoreType.DMA((len(ghosts),)),
        ],
        compiler_params=pltpu.CompilerParams(vmem_limit_bytes=VMEM_KIB * KIB),
        cost_estimate=pl.CostEstimate(flops=500_000_000, bytes_accessed=8 * MIB, transcendentals=0),
        name="diffuse_leaving",
    )(mig_late, counts, mig_sums, mig_coef, *ghosts)


def late_kernel(face_count, cells, lists, counts, coef, early, g0, g1, g2, g3, out_any, out, sums, table, landed, coef_v, coef_s,
                lists_s, counts_s, sem, ghost_sems, coef_sem, list_sems, count_sem, out_sems):
    ghost_copies = start_ghosts((g0, g1, g2, g3), landed, ghost_sems)
    copy = pltpu.make_async_copy(early, sums.at[pl.ds(0, 2 * cells)], sem)
    copy.start()
    count_copy = pltpu.make_async_copy(counts, counts_s, count_sem)
    count_copy.start()
    list_copies = []
    for f in range(face_count):
        part = pltpu.make_async_copy(lists.at[pl.ds(f * LANES, FIRST_LINES)], lists_s.at[f, pl.ds(0, FIRST_LINES)], list_sems.at[f])
        part.start()
        list_copies.append(part)
    lines_of(coef, coef_v, 1.0)
    coef_copy = pltpu.make_async_copy(coef_v, coef_s, coef_sem)
    coef_copy.start()
    spread_ghosts(ghost_copies, landed, table, 0)
    count_copy.wait()
    steps = small_numbers(counts_s[0, 0])
    for part in list_copies:
        part.wait()
    coef_copy.wait()
    flat = coef_s.reshape(coef_s.shape[0] * LANES)
    copy.wait()
    for f in range(face_count):
        weights = flat.at[pl.ds(f * cells, cells + LANES)]
        number = counts_s[f, 0]

        @pl.when(number > FIRST_LINES * BATCH)
        def _():
            rest = LANES - FIRST_LINES
            more = pltpu.make_async_copy(
                lists.at[pl.ds(f * LANES + FIRST_LINES, rest)], lists_s.at[f, pl.ds(FIRST_LINES, rest)], list_sems.at[f])
            more.start()
            more.wait()

        def some(i, carry):
            for j in range(BATCH // GROUP):
                found = []
                of_cells = lists_s.at[f, i, pl.ds(j * GROUP, GROUP)]
                of_rows = lists_s.at[f, i, pl.ds(BATCH + j * GROUP, GROUP)]
                for k in range(GROUP):
                    cell = of_cells[steps[k]]
                    row = rows2(2 * cell)
                    late = table[rows2(of_rows[steps[k]]), :]
                    found.append((row, sums[row, :] + weights[cell] * late))
                for row, value in found:
                    sums[row, :] = value
            return carry

        lax.fori_loop(0, (number + (BATCH - 1)) // BATCH, some, 0)
    span = 256

    def pack(i, carry):
        at = pl.ds(pl.multiple_of(i * span, span), span)
        out[at, 0:LANES] = sums[pl.ds(pl.multiple_of(i * 2 * span, span), span, stride=2), :].astype(BF16)
        out[at, LANES:2 * LANES] = sums[pl.ds(i * 2 * span + 1, span, stride=2), :].astype(BF16)
        return carry

    parts = out_sems.shape[0]
    spans = cells // span // parts
    done = []
    for p in range(parts):
        lax.fori_loop(p * spans, (p + 1) * spans, pack, 0)
        at = pl.ds(p * (cells // parts), cells // parts)
        done.append(pltpu.make_async_copy(out.at[at], out_any.at[at], out_sems.at[p]))
        done[-1].start()
    for part in done:
        part.wait()


def diffuse_late(lists, counts, coef, early, ghosts):
    face_count, cells = coef.shape
    ghost_rows = sum(g.shape[0] for g in ghosts)
    return pl.pallas_call(
        functools.partial(late_kernel, face_count, cells),
        out_shape=jax.ShapeDtypeStruct((cells, 2 * LANES), BF16),
        in_specs=[anywhere(), anywhere(), vmem(), hbm()] + [anywhere()] * len(ghosts),
        out_specs=hbm(),
        scratch_shapes=[
            pltpu.VMEM((cells, 2 * LANES), BF16),
            pltpu.VMEM((2 * cells + 16, LANES), F32),
            pltpu.VMEM((2 * ghost_rows, LANES), F32),
            pltpu.VMEM((len(ghosts),) + ghosts[0].shape, BF16),
            pltpu.VMEM((face_count * cells // LANES + 8, LANES), F32),
            pltpu.SMEM((face_count * cells // LANES + 8, LANES), F32),
            pltpu.SMEM((face_count, LANES, LANES), I32),
            pltpu.SMEM((8, LANES), I32),
            pltpu.SemaphoreType.DMA,
            pltpu.SemaphoreType.DMA((len(ghosts),)),
            pltpu.SemaphoreType.DMA,
            pltpu.SemaphoreType.DMA((face_count,)),
            pltpu.SemaphoreType.DMA,
            pltpu.SemaphoreType.DMA((4,)),
        ],
        compiler_params=pltpu.CompilerParams(vmem_limit_bytes=LESS_VMEM_KIB * KIB),
        cost_estimate=pl.CostEstimate(flops=9_000_000_000, bytes_accessed=24 * MIB, transcendentals=0),
        name="diffuse_late",
    )(lists, counts, coef, early, *ghosts)


def body(dust, classes, kernels, export_ids, faces, face_coef, mig_ids, mig_counts):
    row_width = dust.shape[1]
    export = export_ids.shape[2]
    domains = mig_counts.shape[1]
    capacity = mig_ids.shape[1]
    shift = (8 * export - 1).bit_length()
    own, up, down, left, right = own_cells(dust, classes, kernels, export_ids)
    g0, g1 = passed_along(up, "dx", 1), passed_along(down, "dx", -1)
    g2, g3 = passed_along(left, "dy", 1), passed_along(right, "dy", -1)
    ghosts = (g0, g1, g2, g3)
    faces, face_coef, mig_ids, own = lax.optimization_barrier((faces, face_coef, mig_ids, own))
    mig = mig_ids.T
    early, mig_sums, mig_coef, mig_late, lists, list_counts = diffuse_early(faces, mig, own, face_coef, 4 * export, shift)
    leaving = diffuse_leaving(mig_late, mig_counts, mig_sums, mig_coef, ghosts, face_coef.shape[0])
    arrived = lax.all_to_all(leaving.reshape(domains, capacity, row_width), ("dx", "dy"), split_axis=0, concat_axis=0, tiled=True)
    updated = diffuse_late(lists, list_counts, face_coef, early, ghosts)
    return (updated, arrived.reshape(domains * capacity, row_width))


def solution(mesh):
    return jax.shard_map(
        body,
        mesh=mesh,
        in_specs=(
            P(("dx", "dy"), None),
            P(("dx", "dy")),
            P(),
            P(("dx", "dy"), None, None),
            P(None, ("dx", "dy")),
            P(None, ("dx", "dy")),
            P(("dx", "dy"), None),
            P(("dx", "dy"), None),
        ),
        out_specs=(P(("dx", "dy"), None), P(("dx", "dy"), None)),
        check_vma=False,
    )
```

```python
import functools

import jax
import jax.numpy as jnp
from jax import lax
from jax.experimental import pallas as pl
from jax.experimental.pallas import tpu as pltpu
from jax.sharding import PartitionSpec as P

SUBSTEPS = 6
LANES = 128
GROUP = 8
TILE = 576
CHUNK = 16
BATCH = 32
FIRST_LINES = 4
F32 = jnp.float32
BF16 = jnp.bfloat16
I32 = jnp.int32
KIB = 1 << 10
MIB = 1 << 20
VMEM_KIB = 65330
LESS_VMEM_KIB = 61440


def passed_along(block, axis, distance):
    devices = range(lax.axis_size(axis))
    route = [((i - distance) % len(devices), i) for i in devices]
    return lax.ppermute(block, axis, route)


def iota2(shape, dim):
    return lax.broadcasted_iota(I32, shape, dim)


def small_numbers(none_negative, count=GROUP, apart=1):
    unit = jnp.minimum(none_negative, 0) + apart
    return [unit * k for k in range(count)]


def lines_of(source, lines, times):
    per_row = source.shape[1] // LANES
    for r in range(source.shape[0]):
        for i in range(per_row):
            at = r * per_row + i
            lines[at:at + 1, :] = source[r:r + 1, i * LANES:(i + 1) * LANES] * times


def dot(a, b):
    return jnp.dot(a, b, preferred_element_type=F32)


def rows2(start):
    return pl.ds(pl.multiple_of(start, 2), 2)


def spread_rows(src, table, first, count):
    step = 256

    def one(i, carry):
        block = src[pl.ds(pl.multiple_of(i * step, step), step), :].astype(F32)
        at = 2 * first + i * (2 * step)
        table[pl.ds(pl.multiple_of(at, 8), step, stride=2), :] = block[:, :LANES]
        table[pl.ds(at + 1, step, stride=2), :] = block[:, LANES:]
        return carry

    lax.fori_loop(0, count // step, one, 0)


def class_places(cls, class_count, tile):
    rows = cls.shape[0]
    shift = rows.bit_length() - 1
    wide = class_count * rows
    member = jnp.concatenate([(cls == c).astype(F32) for c in range(class_count)], axis=0)
    member16 = member.astype(BF16)
    before = (iota2((LANES, LANES), 0) < iota2((LANES, LANES), 1)).astype(F32).astype(BF16)
    in_row = dot(member16, before)
    row_total = dot(member16, jnp.ones((LANES, LANES), BF16)).astype(BF16)
    a, b = iota2((wide, wide), 0), iota2((wide, wide), 1)
    same = (a >> shift) == (b >> shift)
    earlier_rows = jnp.logical_and(same, b < a).astype(F32).astype(BF16)
    row_start = dot(earlier_rows, row_total)
    class_total = dot(same.astype(F32).astype(BF16), row_total)
    tiles = ((class_total + (tile - 0.5)) * (1.0 / tile)).astype(I32).astype(F32)
    earlier = jnp.logical_and((b >> shift) < (a >> shift), (b & (rows - 1)) == 0)
    first_tile = dot(earlier.astype(F32).astype(BF16), tiles.astype(BF16))
    place = member * (first_tile * float(tile) + row_start + in_row)
    total = place[:rows]
    for c in range(1, class_count):
        total = total + place[c * rows:(c + 1) * rows]
    last_tile = (first_tile + tiles).astype(I32)
    lane = iota2((8, LANES), 1)
    tile_class = jnp.zeros((8, LANES), I32)
    for c in range(class_count - 1):
        tile_class = tile_class + (last_tile[c * rows:c * rows + 8] <= lane).astype(I32)
    tile_count = last_tile[wide - 8:]
    return (2.0 * total).astype(I32), tile_class, tile_count


def substeps(state, weights):
    one, two = state[:, :LANES], state[:, LANES:]
    bins = float(LANES)
    for _ in range(SUBSTEPS):
        operand = jnp.concatenate([one, two], axis=1).astype(BF16)
        square_one = jnp.sum(one * one, axis=1, keepdims=True)
        square_two = jnp.sum(two * two, axis=1, keepdims=True)
        product = dot(operand, weights)
        one = one + product[:, :LANES] * (1.0 / bins - pl.reciprocal(bins + square_one, approx=True))
        two = two + product[:, LANES:] * (1.0 / bins - pl.reciprocal(bins + square_two, approx=True))
    return one.astype(BF16), two.astype(BF16)


def send_rows(ids, steps, table, outbound, sent, sems, stages):
    span = LANES
    lines = ids.shape[0]

    def pull(line, stage):
        for j in range(span // GROUP):
            group = ids.at[line, pl.ds(j * GROUP, GROUP)]
            for k in range(GROUP):
                stage[rows2((j * GROUP + k) * 2), :] = table[rows2(group[steps[k]]), :]

    def push(block, i, stage):
        at = pl.ds(pl.multiple_of(i * span, span), span)
        block[at, 0:LANES] = stage[pl.ds(0, span, stride=2), :].astype(BF16)
        block[at, LANES:2 * LANES] = stage[pl.ds(1, span, stride=2), :].astype(BF16)

    pull(0, stages[0])
    first = 0
    copies = []
    for number, block in enumerate(outbound):
        spans = block.shape[0] // span

        def pair(i, carry):
            push(block, 2 * i, stages[0])
            pull(first + 2 * i + 1, stages[1])
            push(block, 2 * i + 1, stages[1])
            pull(jnp.minimum(first + 2 * i + 2, lines - 1), stages[0])
            return carry

        lax.fori_loop(0, spans // 2, pair, 0)
        first += spans
        copies.append(pltpu.make_async_copy(block, sent[number], sems.at[number]))
        copies[-1].start()
    for copy in copies:
        copy.wait()


def own_kernel(cells, cls_ref, exp_ref, dust_any, kern_any, out_any, any_up, any_down, any_left, any_right, out_up, out_down,
               out_left, out_right, send_sems, out, dust, kern, sorted_rows, weights, places_v, places, exp_v, exp_s, stage_a, stage_b, sem, dust_sems, kern_sem, exp_sem):
    class_count = kern.shape[0]
    rows = cells // LANES
    parts = dust_sems.shape[0]
    part = cells // parts
    kern_copy = pltpu.make_async_copy(kern_any, kern, kern_sem)
    kern_copy.start()
    dust_copies = []
    for p in range(parts):
        at = pl.ds(p * part, part)
        dust_copies.append(pltpu.make_async_copy(dust_any.at[at], dust.at[at], dust_sems.at[p]))
        dust_copies[-1].start()
    lines_of(exp_ref.at[0], exp_v, 2)
    exp_copy = pltpu.make_async_copy(exp_v, exp_s, exp_sem)
    exp_copy.start()
    place, tile_class, tile_count = class_places(cls_ref[...], class_count, TILE)
    places_v[0:rows, :] = place
    places_v[rows:rows + 8, :] = tile_class
    places_v[rows + 8:rows + 16, :] = tile_count
    copy = pltpu.make_async_copy(places_v, places, sem)
    copy.start()
    zero = jnp.zeros((LANES, LANES), BF16)
    kern_copy.wait()
    for c in range(class_count):
        for s in range(2):
            own = kern[c, s].astype(F32) * float(LANES)
            weights[c, s * LANES:(s + 1) * LANES, s * LANES:(s + 1) * LANES] = own.astype(BF16)
            weights[c, s * LANES:(s + 1) * LANES, (1 - s) * LANES:(2 - s) * LANES] = zero
    for dust_copy in dust_copies:
        dust_copy.wait()
    copy.wait()
    exp_copy.wait()
    steps = small_numbers(places[0, 0])

    def widen(r, stage):
        block = dust[pl.ds(pl.multiple_of(r * LANES, LANES), LANES), :].astype(F32)
        stage[pl.ds(0, LANES, stride=2), :] = block[:, :LANES]
        stage[pl.ds(1, LANES, stride=2), :] = block[:, LANES:]

    def scatter(r, stage):
        for j in range(LANES // GROUP):
            group = places.at[r, pl.ds(j * GROUP, GROUP)]
            for k in range(GROUP):
                sorted_rows[rows2(group[steps[k]]), :] = stage[rows2((j * GROUP + k) * 2), :]

    widen(0, stage_a)

    def pair(i, carry):
        scatter(2 * i, stage_a)
        widen(2 * i + 1, stage_b)
        scatter(2 * i + 1, stage_b)
        widen(jnp.minimum(2 * i + 2, rows - 1), stage_a)
        return carry

    lax.fori_loop(0, rows // 2, pair, 0)

    def tile(i, carry):
        first = i * (2 * TILE)
        at_one = pl.ds(pl.multiple_of(first, 8), TILE, stride=2)
        at_two = pl.ds(first + 1, TILE, stride=2)
        state = jnp.concatenate([sorted_rows[at_one, :], sorted_rows[at_two, :]], axis=1)
        one, two = substeps(state, weights[places[rows, i]])
        sorted_rows[at_one, :] = one.astype(F32)
        sorted_rows[at_two, :] = two.astype(F32)
        return carry

    lax.fori_loop(0, places[rows + 8, 0], tile, 0)

    def gather(r, carry):
        for j in range(LANES // GROUP):
            group = places.at[r, pl.ds(j * GROUP, GROUP)]
            for k in range(GROUP):
                at = (r * LANES + j * GROUP + k) * 2
                out[rows2(at), :] = sorted_rows[rows2(group[steps[k]]), :]
        return carry

    lax.fori_loop(0, rows, gather, 0)
    out_copy = pltpu.make_async_copy(out, out_any, sem)
    out_copy.start()
    send_rows(exp_s, steps, out, (out_up, out_down, out_left, out_right), (any_up, any_down, any_left, any_right), send_sems,
              (stage_a, stage_b))
    out_copy.wait()


def vmem():
    return pl.BlockSpec(memory_space=pltpu.VMEM)


def smem():
    return pl.BlockSpec(memory_space=pltpu.SMEM)


def anywhere():
    return pl.BlockSpec(memory_space=pl.ANY)


def hbm():
    return pl.BlockSpec(memory_space=pltpu.HBM)


def own_cells(dust, classes, kernels, export_ids):
    cells = dust.shape[0]
    export = export_ids.shape[2]
    rows = cells // LANES
    class_count = kernels.shape[0]
    most = cells // TILE + class_count
    block = jax.ShapeDtypeStruct((export, 2 * LANES), BF16)
    return pl.pallas_call(
        functools.partial(own_kernel, cells),
        out_shape=(jax.ShapeDtypeStruct((2 * cells, LANES), F32), block, block, block, block),
        in_specs=[vmem(), vmem(), hbm(), hbm()],
        out_specs=(hbm(), hbm(), hbm(), hbm(), hbm()),
        scratch_shapes=[
            pltpu.VMEM(block.shape, BF16),
            pltpu.VMEM(block.shape, BF16),
            pltpu.VMEM(block.shape, BF16),
            pltpu.VMEM(block.shape, BF16),
            pltpu.SemaphoreType.DMA((4,)),
            pltpu.VMEM((2 * cells, LANES), F32),
            pltpu.VMEM((cells, 2 * LANES), BF16),
            pltpu.VMEM(kernels.shape, BF16),
            pltpu.VMEM((2 * most * TILE, LANES), F32),
            pltpu.VMEM((class_count, 2 * LANES, 2 * LANES), BF16),
            pltpu.VMEM((rows + 16, LANES), I32),
            pltpu.SMEM((rows + 16, LANES), I32),
            pltpu.VMEM((4 * export // LANES, LANES), I32),
            pltpu.SMEM((4 * export // LANES, LANES), I32),
            pltpu.VMEM((2 * LANES, LANES), F32),
            pltpu.VMEM((2 * LANES, LANES), F32),
            pltpu.SemaphoreType.DMA,
            pltpu.SemaphoreType.DMA((4,)),
            pltpu.SemaphoreType.DMA,
            pltpu.SemaphoreType.DMA,
        ],
        compiler_params=pltpu.CompilerParams(vmem_limit_bytes=VMEM_KIB * KIB),
        cost_estimate=pl.CostEstimate(flops=9_000_000_000, bytes_accessed=12 * MIB, transcendentals=0),
        name="coagulate_own",
    )(classes.reshape(rows, LANES), export_ids, dust, kernels)


def pairs(start):
    return pl.ds(pl.multiple_of(start, 8), CHUNK, stride=2), pl.ds(start + 1, CHUNK, stride=2)


def face_sums(own_one, own_two, weights, stage, face_count):
    one, two = own_one, own_two
    for f in range(face_count):
        c = jnp.broadcast_to(weights[:, f:f + 1], (CHUNK, LANES))
        one = one + c * (stage[pl.ds(2 * f * CHUNK, CHUNK, stride=2), :] - own_one)
        two = two + c * (stage[pl.ds(2 * f * CHUNK + 1, CHUNK, stride=2), :] - own_two)
    return one, two


def turn_columns(coef, late, both, columns):
    together = 2
    padded = both.shape[0] // 2
    both[0:coef.shape[0], :] = coef[...]
    both[padded:padded + coef.shape[0], :] = late

    def turn(b, carry):
        for u in range(together):
            at = pl.ds(pl.multiple_of((b * together + u) * LANES, LANES), LANES)
            columns[at, :] = both[:, at].T
        return carry

    lax.fori_loop(0, columns.shape[0] // (LANES * together), turn, 0)


def start_faces(faces, faces_v, faces_s, sems):
    lines_of(faces, faces_v, 2)
    per_face = faces.shape[1] // LANES
    parts = sems.shape[0]
    copies = []
    for p in range(parts):
        copies.append([])
        for f in range(faces.shape[0]):
            at = pl.ds(f * per_face + p * (per_face // parts), per_face // parts)
            copies[p].append(pltpu.make_async_copy(faces_v.at[at], faces_s.at[at], sems.at[p, f]))
            copies[p][f].start()
    return copies


def start_ghosts(ghosts, landed, sems):
    copies = []
    for k, ghost in enumerate(ghosts):
        copies.append(pltpu.make_async_copy(ghost, landed.at[k], sems.at[k]))
        copies[-1].start()
    return copies


def spread_ghosts(copies, landed, table, first):
    for k, copy in enumerate(copies):
        copy.wait()
        spread_rows(landed.at[k], table, first + k * landed.shape[1], landed.shape[1])


def late_lists(face_count, cells, out, out_coef, counts, lines, coef_lines):
    per_face = cells // LANES
    every = face_count * per_face
    shift = per_face.bit_length() - 1
    to = lines[...]
    late = (to >= 2 * cells).astype(F32)
    late16 = late.astype(BF16)
    before = (iota2((LANES, LANES), 0) < iota2((LANES, LANES), 1)).astype(F32).astype(BF16)
    line_total = dot(late16, jnp.ones((LANES, LANES), BF16)).astype(BF16)
    a, b = iota2((every, every), 0), iota2((every, every), 1)
    earlier = jnp.logical_and((a >> shift) == (b >> shift), b < a).astype(F32).astype(BF16)
    line_start = dot(earlier, line_total)
    rank = (dot(late16, before) + line_start).astype(I32)
    place = (iota2((every, LANES), 0) & (per_face - 1)) * LANES + iota2((every, LANES), 1)
    ahead = jnp.where(to >= 2 * cells, place - rank, 0)
    lane = iota2((per_face, LANES), 1)
    where = iota2((per_face, LANES), 0) * LANES + lane

    def from_right(x, digit):
        if digit >= 7:
            return pltpu.roll(x, per_face - (1 << (digit - 7)), 0)
        near = pltpu.roll(x, LANES - (1 << digit), 1)
        return jnp.where(lane < LANES - (1 << digit), near, pltpu.roll(near, per_face - 1, 0))

    for f in range(face_count):
        at = slice(f * per_face, (f + 1) * per_face)
        last = (f + 1) * per_face - 1
        number = (line_start[last:last + 1, :] + line_total[last:last + 1, :].astype(F32)).astype(I32)
        counts[f:f + 1, :] = number
        word = (where << 14) + (to[at] - 2 * cells)
        move = ahead[at]
        weight = coef_lines[at]
        for digit in range(cells.bit_length() - 1):
            next_word, next_move = from_right(word, digit), from_right(move, digit)
            takes = ((next_move >> digit) & 1) == 1
            word = jnp.where(takes, next_word, word)
            weight = jnp.where(takes, from_right(weight, digit), weight)
            move = jnp.where(takes, next_move, jnp.where(((move >> digit) & 1) == 1, 0, move))
        used = where < number
        of_cells = jnp.where(used, (word >> 14) * 2, 2 * cells)
        out_coef[at, :] = jnp.where(used, weight, 0.0)
        of_rows = jnp.where(used, word & ((1 << 14) - 1), 0)
        start = 2 * f * per_face
        rest = per_face - FIRST_LINES
        out[start:start + FIRST_LINES, :] = of_cells[:FIRST_LINES]
        out[start + FIRST_LINES:start + 2 * FIRST_LINES, :] = of_rows[:FIRST_LINES]
        out[start + 2 * FIRST_LINES:start + 2 * FIRST_LINES + rest, :] = of_cells[FIRST_LINES:]
        out[start + 2 * FIRST_LINES + rest:start + 2 * per_face, :] = of_rows[FIRST_LINES:]


def early_kernel(face_count, cells, late_rows, faces_any, mig, mig_counts, own, coef_any, out_any, mig_sums, mig_coef, mig_late, lists,
                 list_coef, counts, out, faces, coef, coef_v, input_sems, table,
                 stage_a, stage_b, both, columns, faces_v, faces_s, sem, face_sem, out_sems):
    inputs = [pltpu.make_async_copy(faces_any, faces, input_sems.at[0]), pltpu.make_async_copy(coef_any, coef, input_sems.at[1])]
    for one in inputs:
        one.start()
    copy = pltpu.make_async_copy(own, table.at[pl.ds(0, 2 * cells)], sem)
    copy.start()
    for one in inputs:
        one.wait()
    face_copies = start_faces(faces, faces_v, faces_s, face_sem)

    def clear(i, carry):
        table[pl.ds(pl.multiple_of(2 * cells + i * 256, 256), 256), :] = jnp.zeros((256, LANES), F32)
        return carry

    lax.fori_loop(0, 2 * late_rows // 256, clear, 0)
    turn_columns(coef, jnp.where(faces[...] >= cells, 2 * (faces[...] - cells), 2 * late_rows).astype(F32), both, columns)
    lines_of(coef, coef_v, 1.0)
    late_lists(face_count, cells, lists, list_coef, counts, faces_v, coef_v)
    for part in face_copies[0]:
        part.wait()
    flat = faces_s.reshape(face_count * cells)
    steps = small_numbers(faces_s[0, 0])
    copy.wait()

    def pull(i, stage):
        for f in range(face_count):
            for j in range(CHUNK // GROUP):
                group = flat.at[pl.ds(i * CHUNK + (f * cells + j * GROUP), GROUP)]
                for k in range(GROUP):
                    stage[rows2((f * CHUNK + j * GROUP + k) * 2), :] = table[rows2(group[steps[k]]), :]

    def push(i, stage):
        at = pairs(i * (2 * CHUNK))
        weights = columns[pl.ds(pl.multiple_of(i * CHUNK, CHUNK), CHUNK), :]
        one, two = face_sums(table[at[0], :], table[at[1], :], weights, stage, face_count)
        out[at[0], :] = one
        out[at[1], :] = two

    pull(0, stage_a)
    chunks = cells // CHUNK

    def pair(i, carry):
        push(2 * i, stage_a)
        pull(2 * i + 1, stage_b)
        push(2 * i + 1, stage_b)
        pull(jnp.minimum(2 * i + 2, chunks - 1), stage_a)
        return carry

    parts = out_sems.shape[0]
    done = []
    for p in range(parts):
        if p + 1 < parts:
            for part in face_copies[p + 1]:
                part.wait()
        lax.fori_loop(p * (chunks // 2 // parts), (p + 1) * (chunks // 2 // parts), pair, 0)
        at = pl.ds(p * (2 * cells // parts), 2 * cells // parts)
        done.append(pltpu.make_async_copy(out.at[at], out_any.at[at], out_sems.at[p]))
        done[-1].start()

    def leaving(i, carry):
        for u in range(CHUNK):
            cell = mig[u, i]
            at = i * CHUNK + u
            mig_sums[rows2(2 * at), :] = out[rows2(2 * cell), :]
            mig_coef[pl.ds(at, 1), :] = columns[pl.ds(cell, 1), :]
        return carry

    lax.fori_loop(0, mig.shape[1], leaving, 0)
    lines = mig_coef.shape[0] // LANES
    padded = both.shape[0] // 2
    for i in range(lines):
        turned = mig_coef[i * LANES:(i + 1) * LANES, :].T.astype(I32)
        for f in range(face_count):
            mig_late[f * lines + i:f * lines + i + 1, :] = turned[padded + f:padded + f + 1, :]
    last = face_count * lines
    mig_late[last:last + 1, 0:mig_counts.shape[1]] = mig_counts[...]
    for part in done:
        part.wait()


def diffuse_early(faces, mig, counts, own, coef, late_rows):
    face_count, cells = coef.shape
    padded = face_count + -face_count % 8
    leaving = mig.shape[0] * mig.shape[1]
    return pl.pallas_call(
        functools.partial(early_kernel, face_count, cells, late_rows),
        out_shape=(
            jax.ShapeDtypeStruct((2 * cells, LANES), F32),
            jax.ShapeDtypeStruct((2 * leaving, LANES), F32),
            jax.ShapeDtypeStruct((leaving, 2 * padded), F32),
            jax.ShapeDtypeStruct((face_count * leaving // LANES + 8, LANES), I32),
            jax.ShapeDtypeStruct((2 * face_count * cells // LANES, LANES), I32),
            jax.ShapeDtypeStruct((face_count * cells // LANES, LANES), F32),
            jax.ShapeDtypeStruct((8, LANES), I32),
        ),
        in_specs=[hbm(), smem(), vmem(), hbm(), hbm()],
        out_specs=(hbm(), vmem(), vmem(), vmem(), vmem(), vmem(), vmem()),
        scratch_shapes=[
            pltpu.VMEM((2 * cells, LANES), F32),
            pltpu.VMEM((face_count, cells), I32),
            pltpu.VMEM((face_count, cells), F32),
            pltpu.VMEM((face_count * cells // LANES, LANES), F32),
            pltpu.SemaphoreType.DMA((2,)),
            pltpu.VMEM((2 * (cells + late_rows), LANES), F32),
            pltpu.VMEM((2 * face_count * CHUNK, LANES), F32),
            pltpu.VMEM((2 * face_count * CHUNK, LANES), F32),
            pltpu.VMEM((2 * padded, cells), F32),
            pltpu.VMEM((cells, 2 * padded), F32),
            pltpu.VMEM((face_count * cells // LANES, LANES), I32),
            pltpu.SMEM((face_count * cells // LANES, LANES), I32),
            pltpu.SemaphoreType.DMA,
            pltpu.SemaphoreType.DMA((4, face_count)),
            pltpu.SemaphoreType.DMA((4,)),
        ],
        compiler_params=pltpu.CompilerParams(vmem_limit_bytes=VMEM_KIB * KIB),
        cost_estimate=pl.CostEstimate(flops=20_000_000_000, bytes_accessed=16 * MIB, transcendentals=0),
        name="diffuse_early",
    )(faces, mig, counts, own, coef)


def leave_kernel(face_count, late_any, sums_any, coef_any, g0, g1, g2, g3, out, table, landed, stage_a, stage_b,
                 late_s, mig_sums, mig_coef, late_sem, sums_sem, coef_sem, ghost_sems):
    ghost_copies = start_ghosts((g0, g1, g2, g3), landed, ghost_sems)
    copies = [
        pltpu.make_async_copy(late_any, late_s, late_sem),
        pltpu.make_async_copy(sums_any, mig_sums, sums_sem),
        pltpu.make_async_copy(coef_any, mig_coef, coef_sem),
    ]
    for copy in copies:
        copy.start()
    ghost_rows = landed.shape[0] * landed.shape[1]
    table[2 * ghost_rows:2 * ghost_rows + 8, :] = jnp.zeros((8, LANES), F32)
    spread_ghosts(ghost_copies, landed, table, 0)
    for copy in copies:
        copy.wait()
    cells = out.shape[0]
    mig_late = late_s.reshape(late_s.shape[0] * LANES)
    steps = small_numbers(late_s[0, 0])
    chunks = cells // CHUNK

    def pull(i, stage):
        for f in range(face_count):
            for j in range(CHUNK // GROUP):
                group = mig_late.at[pl.ds(i * CHUNK + (f * cells + j * GROUP), GROUP)]
                for k in range(GROUP):
                    stage[rows2((f * CHUNK + j * GROUP + k) * 2), :] = table[rows2(group[steps[k]]), :]

    def push(i, stage):
        at = pairs(i * (2 * CHUNK))
        here = pl.ds(pl.multiple_of(i * CHUNK, CHUNK), CHUNK)
        one, two = mig_sums[at[0], :], mig_sums[at[1], :]
        weights = mig_coef[here, :]
        for f in range(face_count):
            c = jnp.broadcast_to(weights[:, f:f + 1], (CHUNK, LANES))
            one = one + c * stage[pl.ds(2 * f * CHUNK, CHUNK, stride=2), :]
            two = two + c * stage[pl.ds(2 * f * CHUNK + 1, CHUNK, stride=2), :]
        keep = iota2((CHUNK, LANES), 0) < mig_late[face_count * cells + i]
        out[here, 0:LANES] = jnp.where(keep, one, 0.0).astype(BF16)
        out[here, LANES:2 * LANES] = jnp.where(keep, two, 0.0).astype(BF16)

    pull(0, stage_a)

    def pair(i, carry):
        push(2 * i, stage_a)
        pull(2 * i + 1, stage_b)
        push(2 * i + 1, stage_b)
        pull(jnp.minimum(2 * i + 2, chunks - 1), stage_a)
        return carry

    lax.fori_loop(0, chunks // 2, pair, 0)


def diffuse_leaving(mig_late, mig_sums, mig_coef, ghosts, face_count):
    ghost_rows = sum(g.shape[0] for g in ghosts)
    return pl.pallas_call(
        functools.partial(leave_kernel, face_count),
        out_shape=jax.ShapeDtypeStruct((mig_coef.shape[0], 2 * LANES), BF16),
        in_specs=[anywhere()] * 7,
        out_specs=vmem(),
        scratch_shapes=[
            pltpu.VMEM((2 * ghost_rows + 8, LANES), F32),
            pltpu.VMEM((len(ghosts),) + ghosts[0].shape, BF16),
            pltpu.VMEM((2 * face_count * CHUNK, LANES), F32),
            pltpu.VMEM((2 * face_count * CHUNK, LANES), F32),
            pltpu.SMEM(mig_late.shape, I32),
            pltpu.VMEM(mig_sums.shape, F32),
            pltpu.VMEM(mig_coef.shape, F32),
            pltpu.SemaphoreType.DMA,
            pltpu.SemaphoreType.DMA,
            pltpu.SemaphoreType.DMA,
            pltpu.SemaphoreType.DMA((len(ghosts),)),
        ],
        compiler_params=pltpu.CompilerParams(vmem_limit_bytes=VMEM_KIB * KIB),
        cost_estimate=pl.CostEstimate(flops=500_000_000, bytes_accessed=8 * MIB, transcendentals=0),
        name="diffuse_leaving",
    )(mig_late, mig_sums, mig_coef, *ghosts)


def late_kernel(face_count, cells, lists, list_coef, counts, early, g0, g1, g2, g3, out_any, out, sums, table, landed, lists_s,
                coef_s, counts_s, sem, ghost_sems, coef_sems, list_sems, count_sem, out_sems):
    ghost_copies = start_ghosts((g0, g1, g2, g3), landed, ghost_sems)
    copy = pltpu.make_async_copy(early, sums.at[pl.ds(0, 2 * cells)], sem)
    copy.start()
    count_copy = pltpu.make_async_copy(counts, counts_s, count_sem)
    count_copy.start()
    list_copies = []
    for f in range(face_count):
        first = pl.ds(2 * f * cells // LANES, 2 * FIRST_LINES)
        part = pltpu.make_async_copy(lists.at[first], lists_s.at[f, pl.ds(0, 2 * FIRST_LINES)], list_sems.at[f])
        part.start()
        list_copies.append(part)
        first = pl.ds(f * cells // LANES, 2 * FIRST_LINES)
        part = pltpu.make_async_copy(list_coef.at[first], coef_s.at[f, pl.ds(0, 2 * FIRST_LINES)], coef_sems.at[f])
        part.start()
        list_copies.append(part)
    spread_ghosts(ghost_copies, landed, table, 0)
    count_copy.wait()
    steps = small_numbers(counts_s[0, 0])
    for part in list_copies:
        part.wait()
    copy.wait()
    for f in range(face_count):
        number = counts_s[f, 0]

        per_line = LANES // BATCH
        line_shift = per_line.bit_length() - 1
        split = FIRST_LINES * per_line
        rest = 2 * cells // LANES - 2 * FIRST_LINES

        def add(cell_line, row_line, coef_line, lane):
            for j in range(BATCH // GROUP):
                found = []
                of_cells = lists_s.at[f, cell_line, pl.ds(lane + j * GROUP, GROUP)]
                of_rows = lists_s.at[f, row_line, pl.ds(lane + j * GROUP, GROUP)]
                weights = coef_s.at[f, coef_line, pl.ds(lane + j * GROUP, GROUP)]
                for k in range(GROUP):
                    row = rows2(of_cells[steps[k]])
                    late = table[rows2(of_rows[steps[k]]), :]
                    found.append((row, sums[row, :] + weights[steps[k]] * late))
                for row, value in found:
                    sums[row, :] = value

        def near(i, carry):
            line = i >> line_shift
            add(line, line + FIRST_LINES, line, (i & (per_line - 1)) * BATCH)
            return carry

        def far(i, carry):
            line = (i >> line_shift) + FIRST_LINES
            add(line, line + rest // 2, line - FIRST_LINES, (i & (per_line - 1)) * BATCH)
            return carry

        batches = (number + (BATCH - 1)) // BATCH
        lax.fori_loop(0, jnp.minimum(batches, split), near, 0)

        @pl.when(batches > split)
        def _():
            at = pl.ds(2 * f * cells // LANES + 2 * FIRST_LINES, rest)
            more = pltpu.make_async_copy(lists.at[at], lists_s.at[f, pl.ds(2 * FIRST_LINES, rest)], list_sems.at[f])
            more.start()
            more.wait()
            rest_coef = cells // LANES - 2 * FIRST_LINES
            at = pl.ds(f * cells // LANES + 2 * FIRST_LINES, rest_coef)
            more = pltpu.make_async_copy(list_coef.at[at], coef_s.at[f, pl.ds(2 * FIRST_LINES, rest_coef)], coef_sems.at[f])
            more.start()
            more.wait()
            lax.fori_loop(split, batches, far, 0)

    span = 256

    def pack(i, carry):
        at = pl.ds(pl.multiple_of(i * span, span), span)
        out[at, 0:LANES] = sums[pl.ds(pl.multiple_of(i * 2 * span, span), span, stride=2), :].astype(BF16)
        out[at, LANES:2 * LANES] = sums[pl.ds(i * 2 * span + 1, span, stride=2), :].astype(BF16)
        return carry

    parts = out_sems.shape[0]
    spans = cells // span // parts
    done = []
    for p in range(parts):
        lax.fori_loop(p * spans, (p + 1) * spans, pack, 0)
        at = pl.ds(p * (cells // parts), cells // parts)
        done.append(pltpu.make_async_copy(out.at[at], out_any.at[at], out_sems.at[p]))
        done[-1].start()
    for part in done:
        part.wait()


def diffuse_late(lists, list_coef, counts, early, ghosts, face_count):
    cells = early.shape[0] // 2
    ghost_rows = sum(g.shape[0] for g in ghosts)
    return pl.pallas_call(
        functools.partial(late_kernel, face_count, cells),
        out_shape=jax.ShapeDtypeStruct((cells, 2 * LANES), BF16),
        in_specs=[hbm(), hbm(), hbm(), hbm()] + [anywhere()] * len(ghosts),
        out_specs=hbm(),
        scratch_shapes=[
            pltpu.VMEM((cells, 2 * LANES), BF16),
            pltpu.VMEM((2 * cells + 16, LANES), F32),
            pltpu.VMEM((2 * ghost_rows, LANES), F32),
            pltpu.VMEM((len(ghosts),) + ghosts[0].shape, BF16),
            pltpu.SMEM((face_count, 2 * cells // LANES, LANES), I32),
            pltpu.SMEM((face_count, cells // LANES, LANES), F32),
            pltpu.SMEM((8, LANES), I32),
            pltpu.SemaphoreType.DMA,
            pltpu.SemaphoreType.DMA((len(ghosts),)),
            pltpu.SemaphoreType.DMA((face_count,)),
            pltpu.SemaphoreType.DMA((face_count,)),
            pltpu.SemaphoreType.DMA,
            pltpu.SemaphoreType.DMA((4,)),
        ],
        compiler_params=pltpu.CompilerParams(vmem_limit_bytes=LESS_VMEM_KIB * KIB),
        cost_estimate=pl.CostEstimate(flops=9_000_000_000, bytes_accessed=24 * MIB, transcendentals=0),
        name="diffuse_late",
    )(lists, list_coef, counts, early, *ghosts)


def body(dust, classes, kernels, export_ids, faces, face_coef, mig_ids, mig_counts):
    row_width = dust.shape[1]
    export = export_ids.shape[2]
    domains = mig_counts.shape[1]
    capacity = mig_ids.shape[1]
    own, up, down, left, right = own_cells(dust, classes, kernels, export_ids)
    g0, g1 = passed_along(up, "dx", 1), passed_along(down, "dx", -1)
    g2, g3 = passed_along(left, "dy", 1), passed_along(right, "dy", -1)
    ghosts = (g0, g1, g2, g3)
    faces, face_coef, mig_ids, own = lax.optimization_barrier((faces, face_coef, mig_ids, own))
    mig = mig_ids.T
    early, mig_sums, mig_coef, mig_late, lists, list_coef, list_counts = diffuse_early(faces, mig, mig_counts, own, face_coef, 4 * export)
    leaving = diffuse_leaving(mig_late, mig_sums, mig_coef, ghosts, face_coef.shape[0])
    arrived = lax.all_to_all(leaving.reshape(domains, capacity, row_width), ("dx", "dy"), split_axis=0, concat_axis=0, tiled=True)
    updated = diffuse_late(lists, list_coef, list_counts, early, ghosts, face_coef.shape[0])
    return (updated, arrived.reshape(domains * capacity, row_width))


def solution(mesh):
    return jax.shard_map(
        body,
        mesh=mesh,
        in_specs=(
            P(("dx", "dy"), None),
            P(("dx", "dy")),
            P(),
            P(("dx", "dy"), None, None),
            P(None, ("dx", "dy")),
            P(None, ("dx", "dy")),
            P(("dx", "dy"), None),
            P(("dx", "dy"), None),
        ),
        out_specs=(P(("dx", "dy"), None), P(("dx", "dy"), None)),
        check_vma=False,
    )
```

```python
import functools

import jax
import jax.numpy as jnp
from jax import lax
from jax.experimental import pallas as pl
from jax.experimental.pallas import tpu as pltpu
from jax.sharding import PartitionSpec as P

SUBSTEPS = 6
LANES = 128
GROUP = 8
TILE = 576
CHUNK = 16
BATCH = 32
FIRST_LINES = 4
F32 = jnp.float32
BF16 = jnp.bfloat16
I32 = jnp.int32
KIB = 1 << 10
MIB = 1 << 20
VMEM_KIB = 65330
LESS_VMEM_KIB = 61440


def passed_along(block, axis, distance):
    devices = range(lax.axis_size(axis))
    route = [((i - distance) % len(devices), i) for i in devices]
    return lax.ppermute(block, axis, route)


def iota2(shape, dim):
    return lax.broadcasted_iota(I32, shape, dim)


def small_numbers(none_negative, count=GROUP, apart=1):
    unit = jnp.minimum(none_negative, 0) + apart
    return [unit * k for k in range(count)]


def lines_of(source, lines, times):
    per_row = source.shape[1] // LANES
    for r in range(source.shape[0]):
        for i in range(per_row):
            at = r * per_row + i
            lines[at:at + 1, :] = source[r:r + 1, i * LANES:(i + 1) * LANES] * times


def dot(a, b):
    return jnp.dot(a, b, preferred_element_type=F32)


def rows2(start):
    return pl.ds(pl.multiple_of(start, 2), 2)


def spread_rows(src, table, first, count):
    step = 256

    def one(i, carry):
        block = src[pl.ds(pl.multiple_of(i * step, step), step), :].astype(F32)
        at = 2 * first + i * (2 * step)
        table[pl.ds(pl.multiple_of(at, 8), step, stride=2), :] = block[:, :LANES]
        table[pl.ds(at + 1, step, stride=2), :] = block[:, LANES:]
        return carry

    lax.fori_loop(0, count // step, one, 0)


def class_places(cls, class_count, tile):
    rows = cls.shape[0]
    shift = rows.bit_length() - 1
    wide = class_count * rows
    member = jnp.concatenate([(cls == c).astype(F32) for c in range(class_count)], axis=0)
    member16 = member.astype(BF16)
    before = (iota2((LANES, LANES), 0) < iota2((LANES, LANES), 1)).astype(F32).astype(BF16)
    in_row = dot(member16, before)
    row_total = dot(member16, jnp.ones((LANES, LANES), BF16)).astype(BF16)
    a, b = iota2((wide, wide), 0), iota2((wide, wide), 1)
    same = (a >> shift) == (b >> shift)
    earlier_rows = jnp.logical_and(same, b < a).astype(F32).astype(BF16)
    row_start = dot(earlier_rows, row_total)
    class_total = dot(same.astype(F32).astype(BF16), row_total)
    tiles = ((class_total + (tile - 0.5)) * (1.0 / tile)).astype(I32).astype(F32)
    earlier = jnp.logical_and((b >> shift) < (a >> shift), (b & (rows - 1)) == 0)
    first_tile = dot(earlier.astype(F32).astype(BF16), tiles.astype(BF16))
    place = member * (first_tile * float(tile) + row_start + in_row)
    total = place[:rows]
    for c in range(1, class_count):
        total = total + place[c * rows:(c + 1) * rows]
    last_tile = (first_tile + tiles).astype(I32)
    lane = iota2((8, LANES), 1)
    tile_class = jnp.zeros((8, LANES), I32)
    for c in range(class_count - 1):
        tile_class = tile_class + (last_tile[c * rows:c * rows + 8] <= lane).astype(I32)
    tile_count = last_tile[wide - 8:]
    return (2.0 * total).astype(I32), tile_class, tile_count


def substeps(state, weights):
    one, two = state[:, :LANES], state[:, LANES:]
    bins = float(LANES)
    for _ in range(SUBSTEPS):
        operand = jnp.concatenate([one, two], axis=1).astype(BF16)
        square_one = jnp.sum(one * one, axis=1, keepdims=True)
        square_two = jnp.sum(two * two, axis=1, keepdims=True)
        product = dot(operand, weights)
        one = one + product[:, :LANES] * (1.0 / bins - pl.reciprocal(bins + square_one, approx=True))
        two = two + product[:, LANES:] * (1.0 / bins - pl.reciprocal(bins + square_two, approx=True))
    return one.astype(BF16), two.astype(BF16)


def send_rows(ids, steps, table, outbound, sent, sems, stages):
    span = LANES
    lines = ids.shape[0]

    def pull(line, stage):
        for j in range(span // GROUP):
            group = ids.at[line, pl.ds(j * GROUP, GROUP)]
            for k in range(GROUP):
                stage[rows2((j * GROUP + k) * 2), :] = table[rows2(group[steps[k]]), :]

    def push(block, i, stage):
        at = pl.ds(pl.multiple_of(i * span, span), span)
        block[at, 0:LANES] = stage[pl.ds(0, span, stride=2), :].astype(BF16)
        block[at, LANES:2 * LANES] = stage[pl.ds(1, span, stride=2), :].astype(BF16)

    pull(0, stages[0])
    first = 0
    copies = []
    for number, block in enumerate(outbound):
        spans = block.shape[0] // span

        def pair(i, carry):
            push(block, 2 * i, stages[0])
            pull(first + 2 * i + 1, stages[1])
            push(block, 2 * i + 1, stages[1])
            pull(jnp.minimum(first + 2 * i + 2, lines - 1), stages[0])
            return carry

        lax.fori_loop(0, spans // 2, pair, 0)
        first += spans
        copies.append(pltpu.make_async_copy(block, sent[number], sems.at[number]))
        copies[-1].start()
    for copy in copies:
        copy.wait()


def own_kernel(cells, cls_ref, exp_ref, dust_any, kern_any, out_any, any_up, any_down, any_left, any_right, out_up, out_down,
               out_left, out_right, send_sems, out, dust, kern, sorted_rows, weights, places_v, places, exp_v, exp_s, stage_a, stage_b, sem, dust_sems, kern_sem, exp_sem):
    class_count = kern.shape[0]
    rows = cells // LANES
    parts = dust_sems.shape[0]
    part = cells // parts
    kern_copy = pltpu.make_async_copy(kern_any, kern, kern_sem)
    kern_copy.start()
    dust_copies = []
    for p in range(parts):
        at = pl.ds(p * part, part)
        dust_copies.append(pltpu.make_async_copy(dust_any.at[at], dust.at[at], dust_sems.at[p]))
        dust_copies[-1].start()
    lines_of(exp_ref.at[0], exp_v, 2)
    exp_copy = pltpu.make_async_copy(exp_v, exp_s, exp_sem)
    exp_copy.start()
    place, tile_class, tile_count = class_places(cls_ref[...], class_count, TILE)
    places_v[0:rows, :] = place
    places_v[rows:rows + 8, :] = tile_class
    places_v[rows + 8:rows + 16, :] = tile_count
    copy = pltpu.make_async_copy(places_v, places, sem)
    copy.start()
    zero = jnp.zeros((LANES, LANES), BF16)
    kern_copy.wait()
    for c in range(class_count):
        for s in range(2):
            own = kern[c, s].astype(F32) * float(LANES)
            weights[c, s * LANES:(s + 1) * LANES, s * LANES:(s + 1) * LANES] = own.astype(BF16)
            weights[c, s * LANES:(s + 1) * LANES, (1 - s) * LANES:(2 - s) * LANES] = zero
    for dust_copy in dust_copies:
        dust_copy.wait()
    copy.wait()
    exp_copy.wait()
    steps = small_numbers(places[0, 0])

    def widen(r, stage):
        block = dust[pl.ds(pl.multiple_of(r * LANES, LANES), LANES), :].astype(F32)
        stage[pl.ds(0, LANES, stride=2), :] = block[:, :LANES]
        stage[pl.ds(1, LANES, stride=2), :] = block[:, LANES:]

    def scatter(r, stage):
        for j in range(LANES // GROUP):
            group = places.at[r, pl.ds(j * GROUP, GROUP)]
            for k in range(GROUP):
                sorted_rows[rows2(group[steps[k]]), :] = stage[rows2((j * GROUP + k) * 2), :]

    widen(0, stage_a)

    def pair(i, carry):
        scatter(2 * i, stage_a)
        widen(2 * i + 1, stage_b)
        scatter(2 * i + 1, stage_b)
        widen(jnp.minimum(2 * i + 2, rows - 1), stage_a)
        return carry

    lax.fori_loop(0, rows // 2, pair, 0)

    def tile(i, carry):
        first = i * (2 * TILE)
        at_one = pl.ds(pl.multiple_of(first, 8), TILE, stride=2)
        at_two = pl.ds(first + 1, TILE, stride=2)
        state = jnp.concatenate([sorted_rows[at_one, :], sorted_rows[at_two, :]], axis=1)
        one, two = substeps(state, weights[places[rows, i]])
        sorted_rows[at_one, :] = one.astype(F32)
        sorted_rows[at_two, :] = two.astype(F32)
        return carry

    lax.fori_loop(0, places[rows + 8, 0], tile, 0)

    def gather(r, carry):
        for j in range(LANES // GROUP):
            group = places.at[r, pl.ds(j * GROUP, GROUP)]
            for k in range(GROUP):
                at = (r * LANES + j * GROUP + k) * 2
                out[rows2(at), :] = sorted_rows[rows2(group[steps[k]]), :]
        return carry

    lax.fori_loop(0, rows, gather, 0)
    out_copy = pltpu.make_async_copy(out, out_any, sem)
    out_copy.start()
    send_rows(exp_s, steps, out, (out_up, out_down, out_left, out_right), (any_up, any_down, any_left, any_right), send_sems,
              (stage_a, stage_b))
    out_copy.wait()


def vmem():
    return pl.BlockSpec(memory_space=pltpu.VMEM)


def smem():
    return pl.BlockSpec(memory_space=pltpu.SMEM)


def anywhere():
    return pl.BlockSpec(memory_space=pl.ANY)


def hbm():
    return pl.BlockSpec(memory_space=pltpu.HBM)


def own_cells(dust, classes, kernels, export_ids):
    cells = dust.shape[0]
    export = export_ids.shape[2]
    rows = cells // LANES
    class_count = kernels.shape[0]
    most = cells // TILE + class_count
    block = jax.ShapeDtypeStruct((export, 2 * LANES), BF16)
    return pl.pallas_call(
        functools.partial(own_kernel, cells),
        out_shape=(jax.ShapeDtypeStruct((2 * cells, LANES), F32), block, block, block, block),
        in_specs=[vmem(), vmem(), hbm(), hbm()],
        out_specs=(hbm(), hbm(), hbm(), hbm(), hbm()),
        scratch_shapes=[
            pltpu.VMEM(block.shape, BF16),
            pltpu.VMEM(block.shape, BF16),
            pltpu.VMEM(block.shape, BF16),
            pltpu.VMEM(block.shape, BF16),
            pltpu.SemaphoreType.DMA((4,)),
            pltpu.VMEM((2 * cells, LANES), F32),
            pltpu.VMEM((cells, 2 * LANES), BF16),
            pltpu.VMEM(kernels.shape, BF16),
            pltpu.VMEM((2 * most * TILE + 8, LANES), F32),
            pltpu.VMEM((class_count, 2 * LANES, 2 * LANES), BF16),
            pltpu.VMEM((rows + 16, LANES), I32),
            pltpu.SMEM((rows + 16, LANES), I32),
            pltpu.VMEM((4 * export // LANES, LANES), I32),
            pltpu.SMEM((4 * export // LANES, LANES), I32),
            pltpu.VMEM((2 * LANES + 8, LANES), F32),
            pltpu.VMEM((2 * LANES + 8, LANES), F32),
            pltpu.SemaphoreType.DMA,
            pltpu.SemaphoreType.DMA((4,)),
            pltpu.SemaphoreType.DMA,
            pltpu.SemaphoreType.DMA,
        ],
        compiler_params=pltpu.CompilerParams(vmem_limit_bytes=VMEM_KIB * KIB),
        cost_estimate=pl.CostEstimate(flops=9_000_000_000, bytes_accessed=12 * MIB, transcendentals=0),
        name="coagulate_own",
    )(classes.reshape(rows, LANES), export_ids, dust, kernels)


def pairs(start):
    return pl.ds(pl.multiple_of(start, 8), CHUNK, stride=2), pl.ds(start + 1, CHUNK, stride=2)


def face_sums(own_one, own_two, weights, stage, face_count):
    one, two = own_one, own_two
    for f in range(face_count):
        c = jnp.broadcast_to(weights[:, f:f + 1], (CHUNK, LANES))
        one = one + c * (stage[pl.ds(2 * f * CHUNK, CHUNK, stride=2), :] - own_one)
        two = two + c * (stage[pl.ds(2 * f * CHUNK + 1, CHUNK, stride=2), :] - own_two)
    return one, two


def turn_columns(coef, late, both, columns):
    together = 2
    padded = both.shape[0] // 2
    both[0:coef.shape[0], :] = coef[...]
    both[padded:padded + coef.shape[0], :] = late

    def turn(b, carry):
        for u in range(together):
            at = pl.ds(pl.multiple_of((b * together + u) * LANES, LANES), LANES)
            columns[at, :] = both[:, at].T
        return carry

    lax.fori_loop(0, columns.shape[0] // (LANES * together), turn, 0)


def start_faces(faces, faces_v, faces_s, sems):
    lines_of(faces, faces_v, 2)
    per_face = faces.shape[1] // LANES
    parts = sems.shape[0]
    copies = []
    for p in range(parts):
        copies.append([])
        for f in range(faces.shape[0]):
            at = pl.ds(f * per_face + p * (per_face // parts), per_face // parts)
            copies[p].append(pltpu.make_async_copy(faces_v.at[at], faces_s.at[at], sems.at[p, f]))
            copies[p][f].start()
    return copies


def start_ghosts(ghosts, landed, sems):
    copies = []
    for k, ghost in enumerate(ghosts):
        copies.append(pltpu.make_async_copy(ghost, landed.at[k], sems.at[k]))
        copies[-1].start()
    return copies


def spread_ghosts(copies, landed, table, first):
    for k, copy in enumerate(copies):
        copy.wait()
        spread_rows(landed.at[k], table, first + k * landed.shape[1], landed.shape[1])


def late_lists(face_count, cells, out, out_coef, counts, lines, coef_lines):
    per_face = cells // LANES
    every = face_count * per_face
    shift = per_face.bit_length() - 1
    to = lines[...]
    late = (to >= 2 * cells).astype(F32)
    late16 = late.astype(BF16)
    before = (iota2((LANES, LANES), 0) < iota2((LANES, LANES), 1)).astype(F32).astype(BF16)
    line_total = dot(late16, jnp.ones((LANES, LANES), BF16)).astype(BF16)
    a, b = iota2((every, every), 0), iota2((every, every), 1)
    earlier = jnp.logical_and((a >> shift) == (b >> shift), b < a).astype(F32).astype(BF16)
    line_start = dot(earlier, line_total)
    rank = (dot(late16, before) + line_start).astype(I32)
    place = (iota2((every, LANES), 0) & (per_face - 1)) * LANES + iota2((every, LANES), 1)
    ahead = jnp.where(to >= 2 * cells, place - rank, 0)
    lane = iota2((per_face, LANES), 1)
    where = iota2((per_face, LANES), 0) * LANES + lane

    def from_right(x, digit):
        if digit >= 7:
            return pltpu.roll(x, per_face - (1 << (digit - 7)), 0)
        near = pltpu.roll(x, LANES - (1 << digit), 1)
        return jnp.where(lane < LANES - (1 << digit), near, pltpu.roll(near, per_face - 1, 0))

    for f in range(face_count):
        at = slice(f * per_face, (f + 1) * per_face)
        last = (f + 1) * per_face - 1
        number = (line_start[last:last + 1, :] + line_total[last:last + 1, :].astype(F32)).astype(I32)
        counts[f:f + 1, :] = number
        word = (where << 14) + (to[at] - 2 * cells)
        move = ahead[at]
        weight = coef_lines[at]
        for digit in range(cells.bit_length() - 1):
            next_word, next_move = from_right(word, digit), from_right(move, digit)
            takes = ((next_move >> digit) & 1) == 1
            word = jnp.where(takes, next_word, word)
            weight = jnp.where(takes, from_right(weight, digit), weight)
            move = jnp.where(takes, next_move, jnp.where(((move >> digit) & 1) == 1, 0, move))
        used = where < number
        of_cells = jnp.where(used, (word >> 14) * 2, 2 * cells)
        out_coef[at, :] = jnp.where(used, weight, 0.0)
        of_rows = jnp.where(used, word & ((1 << 14) - 1), 0)
        start = 2 * f * per_face
        rest = per_face - FIRST_LINES
        out[start:start + FIRST_LINES, :] = of_cells[:FIRST_LINES]
        out[start + FIRST_LINES:start + 2 * FIRST_LINES, :] = of_rows[:FIRST_LINES]
        out[start + 2 * FIRST_LINES:start + 2 * FIRST_LINES + rest, :] = of_cells[FIRST_LINES:]
        out[start + 2 * FIRST_LINES + rest:start + 2 * per_face, :] = of_rows[FIRST_LINES:]


def early_kernel(face_count, cells, late_rows, faces_any, mig, mig_counts, own, coef_any, out_any, mig_sums, mig_coef, mig_late, lists,
                 list_coef, counts, out, faces, coef, coef_v, input_sems, table,
                 stage_a, stage_b, both, columns, faces_v, faces_s, sem, face_sem, out_sems):
    inputs = [pltpu.make_async_copy(faces_any, faces, input_sems.at[0]), pltpu.make_async_copy(coef_any, coef, input_sems.at[1])]
    for one in inputs:
        one.start()
    copy = pltpu.make_async_copy(own, table.at[pl.ds(0, 2 * cells)], sem)
    copy.start()
    for one in inputs:
        one.wait()
    face_copies = start_faces(faces, faces_v, faces_s, face_sem)

    def clear(i, carry):
        table[pl.ds(pl.multiple_of(2 * cells + i * 256, 256), 256), :] = jnp.zeros((256, LANES), F32)
        return carry

    lax.fori_loop(0, 2 * late_rows // 256, clear, 0)
    turn_columns(coef, jnp.where(faces[...] >= cells, 2 * (faces[...] - cells), 2 * late_rows).astype(F32), both, columns)
    lines_of(coef, coef_v, 1.0)
    late_lists(face_count, cells, lists, list_coef, counts, faces_v, coef_v)
    for part in face_copies[0]:
        part.wait()
    flat = faces_s.reshape(face_count * cells)
    steps = small_numbers(faces_s[0, 0])
    copy.wait()

    def pull(i, stage):
        for f in range(face_count):
            for j in range(CHUNK // GROUP):
                group = flat.at[pl.ds(i * CHUNK + (f * cells + j * GROUP), GROUP)]
                for k in range(GROUP):
                    stage[rows2((f * CHUNK + j * GROUP + k) * 2), :] = table[rows2(group[steps[k]]), :]

    def push(i, stage):
        at = pairs(i * (2 * CHUNK))
        weights = columns[pl.ds(pl.multiple_of(i * CHUNK, CHUNK), CHUNK), :]
        one, two = face_sums(table[at[0], :], table[at[1], :], weights, stage, face_count)
        out[at[0], :] = one
        out[at[1], :] = two

    pull(0, stage_a)
    chunks = cells // CHUNK

    def pair(i, carry):
        push(2 * i, stage_a)
        pull(2 * i + 1, stage_b)
        push(2 * i + 1, stage_b)
        pull(jnp.minimum(2 * i + 2, chunks - 1), stage_a)
        return carry

    parts = out_sems.shape[0]
    done = []
    for p in range(parts):
        if p + 1 < parts:
            for part in face_copies[p + 1]:
                part.wait()
        lax.fori_loop(p * (chunks // 2 // parts), (p + 1) * (chunks // 2 // parts), pair, 0)
        at = pl.ds(p * (2 * cells // parts), 2 * cells // parts)
        done.append(pltpu.make_async_copy(out.at[at], out_any.at[at], out_sems.at[p]))
        done[-1].start()

    def leaving(i, carry):
        for u in range(CHUNK):
            cell = mig[u, i]
            at = i * CHUNK + u
            mig_sums[rows2(2 * at), :] = out[rows2(2 * cell), :]
            mig_coef[pl.ds(at, 1), :] = columns[pl.ds(cell, 1), :]
        return carry

    lax.fori_loop(0, mig.shape[1], leaving, 0)
    lines = mig_coef.shape[0] // LANES
    padded = both.shape[0] // 2
    for i in range(lines):
        turned = mig_coef[i * LANES:(i + 1) * LANES, :].T.astype(I32)
        for f in range(face_count):
            mig_late[f * lines + i:f * lines + i + 1, :] = turned[padded + f:padded + f + 1, :]
    last = face_count * lines
    mig_late[last:last + 1, 0:mig_counts.shape[1]] = mig_counts[...]
    for part in done:
        part.wait()


def diffuse_early(faces, mig, counts, own, coef, late_rows):
    face_count, cells = coef.shape
    padded = face_count + -face_count % 8
    leaving = mig.shape[0] * mig.shape[1]
    return pl.pallas_call(
        functools.partial(early_kernel, face_count, cells, late_rows),
        out_shape=(
            jax.ShapeDtypeStruct((2 * cells, LANES), F32),
            jax.ShapeDtypeStruct((2 * leaving, LANES), F32),
            jax.ShapeDtypeStruct((leaving, 2 * padded), F32),
            jax.ShapeDtypeStruct((face_count * leaving // LANES + 8, LANES), I32),
            jax.ShapeDtypeStruct((2 * face_count * cells // LANES, LANES), I32),
            jax.ShapeDtypeStruct((face_count * cells // LANES, LANES), F32),
            jax.ShapeDtypeStruct((8, LANES), I32),
        ),
        in_specs=[hbm(), smem(), vmem(), hbm(), hbm()],
        out_specs=(hbm(), vmem(), vmem(), vmem(), vmem(), vmem(), vmem()),
        scratch_shapes=[
            pltpu.VMEM((2 * cells + 8, LANES), F32),
            pltpu.VMEM((face_count, cells), I32),
            pltpu.VMEM((face_count, cells), F32),
            pltpu.VMEM((face_count * cells // LANES, LANES), F32),
            pltpu.SemaphoreType.DMA((2,)),
            pltpu.VMEM((2 * (cells + late_rows), LANES), F32),
            pltpu.VMEM((2 * face_count * CHUNK + 8, LANES), F32),
            pltpu.VMEM((2 * face_count * CHUNK + 8, LANES), F32),
            pltpu.VMEM((2 * padded, cells), F32),
            pltpu.VMEM((cells, 2 * padded), F32),
            pltpu.VMEM((face_count * cells // LANES, LANES), I32),
            pltpu.SMEM((face_count * cells // LANES, LANES), I32),
            pltpu.SemaphoreType.DMA,
            pltpu.SemaphoreType.DMA((4, face_count)),
            pltpu.SemaphoreType.DMA((4,)),
        ],
        compiler_params=pltpu.CompilerParams(vmem_limit_bytes=VMEM_KIB * KIB),
        cost_estimate=pl.CostEstimate(flops=20_000_000_000, bytes_accessed=16 * MIB, transcendentals=0),
        name="diffuse_early",
    )(faces, mig, counts, own, coef)


def leave_kernel(face_count, late_any, sums_any, coef_any, g0, g1, g2, g3, out, table, landed, stage_a, stage_b,
                 late_s, mig_sums, mig_coef, late_sem, sums_sem, coef_sem, ghost_sems):
    ghost_copies = start_ghosts((g0, g1, g2, g3), landed, ghost_sems)
    copies = [
        pltpu.make_async_copy(late_any, late_s, late_sem),
        pltpu.make_async_copy(sums_any, mig_sums.at[pl.ds(0, sums_any.shape[0])], sums_sem),
        pltpu.make_async_copy(coef_any, mig_coef, coef_sem),
    ]
    for copy in copies:
        copy.start()
    ghost_rows = landed.shape[0] * landed.shape[1]
    table[2 * ghost_rows:2 * ghost_rows + 8, :] = jnp.zeros((8, LANES), F32)
    spread_ghosts(ghost_copies, landed, table, 0)
    for copy in copies:
        copy.wait()
    cells = out.shape[0]
    mig_late = late_s.reshape(late_s.shape[0] * LANES)
    steps = small_numbers(late_s[0, 0])
    chunks = cells // CHUNK

    def pull(i, stage):
        for f in range(face_count):
            for j in range(CHUNK // GROUP):
                group = mig_late.at[pl.ds(i * CHUNK + (f * cells + j * GROUP), GROUP)]
                for k in range(GROUP):
                    stage[rows2((f * CHUNK + j * GROUP + k) * 2), :] = table[rows2(group[steps[k]]), :]

    def push(i, stage):
        at = pairs(i * (2 * CHUNK))
        here = pl.ds(pl.multiple_of(i * CHUNK, CHUNK), CHUNK)
        one, two = mig_sums[at[0], :], mig_sums[at[1], :]
        weights = mig_coef[here, :]
        for f in range(face_count):
            c = jnp.broadcast_to(weights[:, f:f + 1], (CHUNK, LANES))
            one = one + c * stage[pl.ds(2 * f * CHUNK, CHUNK, stride=2), :]
            two = two + c * stage[pl.ds(2 * f * CHUNK + 1, CHUNK, stride=2), :]
        keep = iota2((CHUNK, LANES), 0) < mig_late[face_count * cells + i]
        out[here, 0:LANES] = jnp.where(keep, one, 0.0).astype(BF16)
        out[here, LANES:2 * LANES] = jnp.where(keep, two, 0.0).astype(BF16)

    pull(0, stage_a)

    def pair(i, carry):
        push(2 * i, stage_a)
        pull(2 * i + 1, stage_b)
        push(2 * i + 1, stage_b)
        pull(jnp.minimum(2 * i + 2, chunks - 1), stage_a)
        return carry

    lax.fori_loop(0, chunks // 2, pair, 0)


def diffuse_leaving(mig_late, mig_sums, mig_coef, ghosts, face_count):
    ghost_rows = sum(g.shape[0] for g in ghosts)
    return pl.pallas_call(
        functools.partial(leave_kernel, face_count),
        out_shape=jax.ShapeDtypeStruct((mig_coef.shape[0], 2 * LANES), BF16),
        in_specs=[anywhere()] * 7,
        out_specs=vmem(),
        scratch_shapes=[
            pltpu.VMEM((2 * ghost_rows + 8, LANES), F32),
            pltpu.VMEM((len(ghosts),) + ghosts[0].shape, BF16),
            pltpu.VMEM((2 * face_count * CHUNK + 8, LANES), F32),
            pltpu.VMEM((2 * face_count * CHUNK + 8, LANES), F32),
            pltpu.SMEM(mig_late.shape, I32),
            pltpu.VMEM((mig_sums.shape[0] + 8, LANES), F32),
            pltpu.VMEM(mig_coef.shape, F32),
            pltpu.SemaphoreType.DMA,
            pltpu.SemaphoreType.DMA,
            pltpu.SemaphoreType.DMA,
            pltpu.SemaphoreType.DMA((len(ghosts),)),
        ],
        compiler_params=pltpu.CompilerParams(vmem_limit_bytes=VMEM_KIB * KIB),
        cost_estimate=pl.CostEstimate(flops=500_000_000, bytes_accessed=8 * MIB, transcendentals=0),
        name="diffuse_leaving",
    )(mig_late, mig_sums, mig_coef, *ghosts)


def late_kernel(face_count, cells, lists, list_coef, counts, early, g0, g1, g2, g3, out_any, out, sums, table, landed, lists_s,
                coef_s, counts_s, sem, ghost_sems, coef_sems, list_sems, count_sem, out_sems):
    ghost_copies = start_ghosts((g0, g1, g2, g3), landed, ghost_sems)
    copy = pltpu.make_async_copy(early, sums.at[pl.ds(0, 2 * cells)], sem)
    copy.start()
    count_copy = pltpu.make_async_copy(counts, counts_s, count_sem)
    count_copy.start()
    list_copies = []
    for f in range(face_count):
        first = pl.ds(2 * f * cells // LANES, 2 * FIRST_LINES)
        part = pltpu.make_async_copy(lists.at[first], lists_s.at[f, pl.ds(0, 2 * FIRST_LINES)], list_sems.at[f])
        part.start()
        list_copies.append(part)
        first = pl.ds(f * cells // LANES, 2 * FIRST_LINES)
        part = pltpu.make_async_copy(list_coef.at[first], coef_s.at[f, pl.ds(0, 2 * FIRST_LINES)], coef_sems.at[f])
        part.start()
        list_copies.append(part)
    spread_ghosts(ghost_copies, landed, table, 0)
    count_copy.wait()
    steps = small_numbers(counts_s[0, 0])
    for part in list_copies:
        part.wait()
    copy.wait()
    for f in range(face_count):
        number = counts_s[f, 0]

        per_line = LANES // BATCH
        line_shift = per_line.bit_length() - 1
        split = FIRST_LINES * per_line
        rest = 2 * cells // LANES - 2 * FIRST_LINES

        def add(cell_line, row_line, coef_line, lane):
            for j in range(BATCH // GROUP):
                found = []
                of_cells = lists_s.at[f, cell_line, pl.ds(lane + j * GROUP, GROUP)]
                of_rows = lists_s.at[f, row_line, pl.ds(lane + j * GROUP, GROUP)]
                weights = coef_s.at[f, coef_line, pl.ds(lane + j * GROUP, GROUP)]
                for k in range(GROUP):
                    row = rows2(of_cells[steps[k]])
                    late = table[rows2(of_rows[steps[k]]), :]
                    found.append((row, sums[row, :] + weights[steps[k]] * late))
                for row, value in found:
                    sums[row, :] = value

        def near(i, carry):
            line = i >> line_shift
            add(line, line + FIRST_LINES, line, (i & (per_line - 1)) * BATCH)
            return carry

        def far(i, carry):
            line = (i >> line_shift) + FIRST_LINES
            add(line, line + rest // 2, line - FIRST_LINES, (i & (per_line - 1)) * BATCH)
            return carry

        batches = (number + (BATCH - 1)) // BATCH
        lax.fori_loop(0, jnp.minimum(batches, split), near, 0)

        @pl.when(batches > split)
        def _():
            at = pl.ds(2 * f * cells // LANES + 2 * FIRST_LINES, rest)
            more = pltpu.make_async_copy(lists.at[at], lists_s.at[f, pl.ds(2 * FIRST_LINES, rest)], list_sems.at[f])
            more.start()
            more.wait()
            rest_coef = cells // LANES - 2 * FIRST_LINES
            at = pl.ds(f * cells // LANES + 2 * FIRST_LINES, rest_coef)
            more = pltpu.make_async_copy(list_coef.at[at], coef_s.at[f, pl.ds(2 * FIRST_LINES, rest_coef)], coef_sems.at[f])
            more.start()
            more.wait()
            lax.fori_loop(split, batches, far, 0)

    span = 256

    def pack(i, carry):
        at = pl.ds(pl.multiple_of(i * span, span), span)
        out[at, 0:LANES] = sums[pl.ds(pl.multiple_of(i * 2 * span, span), span, stride=2), :].astype(BF16)
        out[at, LANES:2 * LANES] = sums[pl.ds(i * 2 * span + 1, span, stride=2), :].astype(BF16)
        return carry

    parts = out_sems.shape[0]
    spans = cells // span // parts
    done = []
    for p in range(parts):
        lax.fori_loop(p * spans, (p + 1) * spans, pack, 0)
        at = pl.ds(p * (cells // parts), cells // parts)
        done.append(pltpu.make_async_copy(out.at[at], out_any.at[at], out_sems.at[p]))
        done[-1].start()
    for part in done:
        part.wait()


def diffuse_late(lists, list_coef, counts, early, ghosts, face_count):
    cells = early.shape[0] // 2
    ghost_rows = sum(g.shape[0] for g in ghosts)
    return pl.pallas_call(
        functools.partial(late_kernel, face_count, cells),
        out_shape=jax.ShapeDtypeStruct((cells, 2 * LANES), BF16),
        in_specs=[hbm(), hbm(), hbm(), hbm()] + [anywhere()] * len(ghosts),
        out_specs=hbm(),
        scratch_shapes=[
            pltpu.VMEM((cells, 2 * LANES), BF16),
            pltpu.VMEM((2 * cells + 16, LANES), F32),
            pltpu.VMEM((2 * ghost_rows + 8, LANES), F32),
            pltpu.VMEM((len(ghosts),) + ghosts[0].shape, BF16),
            pltpu.SMEM((face_count, 2 * cells // LANES, LANES), I32),
            pltpu.SMEM((face_count, cells // LANES, LANES), F32),
            pltpu.SMEM((8, LANES), I32),
            pltpu.SemaphoreType.DMA,
            pltpu.SemaphoreType.DMA((len(ghosts),)),
            pltpu.SemaphoreType.DMA((face_count,)),
            pltpu.SemaphoreType.DMA((face_count,)),
            pltpu.SemaphoreType.DMA,
            pltpu.SemaphoreType.DMA((8,)),
        ],
        compiler_params=pltpu.CompilerParams(vmem_limit_bytes=LESS_VMEM_KIB * KIB),
        cost_estimate=pl.CostEstimate(flops=9_000_000_000, bytes_accessed=24 * MIB, transcendentals=0),
        name="diffuse_late",
    )(lists, list_coef, counts, early, *ghosts)


def body(dust, classes, kernels, export_ids, faces, face_coef, mig_ids, mig_counts):
    row_width = dust.shape[1]
    export = export_ids.shape[2]
    domains = mig_counts.shape[1]
    capacity = mig_ids.shape[1]
    own, up, down, left, right = own_cells(dust, classes, kernels, export_ids)
    g0, g1 = passed_along(up, "dx", 1), passed_along(down, "dx", -1)
    g2, g3 = passed_along(left, "dy", 1), passed_along(right, "dy", -1)
    ghosts = (g0, g1, g2, g3)
    faces, face_coef, mig_ids, own = lax.optimization_barrier((faces, face_coef, mig_ids, own))
    mig = mig_ids.T
    early, mig_sums, mig_coef, mig_late, lists, list_coef, list_counts = diffuse_early(faces, mig, mig_counts, own, face_coef, 4 * export)
    leaving = diffuse_leaving(mig_late, mig_sums, mig_coef, ghosts, face_coef.shape[0])
    arrived = lax.all_to_all(leaving.reshape(domains, capacity, row_width), ("dx", "dy"), split_axis=0, concat_axis=0, tiled=True)
    updated = diffuse_late(lists, list_coef, list_counts, early, ghosts, face_coef.shape[0])
    return (updated, arrived.reshape(domains * capacity, row_width))


def solution(mesh):
    return jax.shard_map(
        body,
        mesh=mesh,
        in_specs=(
            P(("dx", "dy"), None),
            P(("dx", "dy")),
            P(),
            P(("dx", "dy"), None, None),
            P(None, ("dx", "dy")),
            P(None, ("dx", "dy")),
            P(("dx", "dy"), None),
            P(("dx", "dy"), None),
        ),
        out_specs=(P(("dx", "dy"), None), P(("dx", "dy"), None)),
        check_vma=False,
    )
```

```python
import functools

import jax
import jax.numpy as jnp
from jax import lax
from jax.experimental import pallas as pl
from jax.experimental.pallas import tpu as pltpu
from jax.sharding import PartitionSpec as P

SUBSTEPS = 6
LANES = 128
GROUP = 8
TILE = 576
CHUNK = 16
BATCH = 32
FIRST_LINES = 4
F32 = jnp.float32
BF16 = jnp.bfloat16
I32 = jnp.int32
KIB = 1 << 10
MIB = 1 << 20
VMEM_KIB = 65330
LESS_VMEM_KIB = 61440


def passed_along(block, axis, distance):
    devices = range(lax.axis_size(axis))
    route = [((i - distance) % len(devices), i) for i in devices]
    return lax.ppermute(block, axis, route)


def iota2(shape, dim):
    return lax.broadcasted_iota(I32, shape, dim)


def small_numbers(none_negative, count=GROUP, apart=1):
    unit = jnp.minimum(none_negative, 0) + apart
    return [unit * k for k in range(count)]


def lines_of(source, lines, times):
    per_row = source.shape[1] // LANES
    for r in range(source.shape[0]):
        for i in range(per_row):
            at = r * per_row + i
            lines[at:at + 1, :] = source[r:r + 1, i * LANES:(i + 1) * LANES] * times


def dot(a, b):
    return jnp.dot(a, b, preferred_element_type=F32)


def rows2(start):
    return pl.ds(pl.multiple_of(start, 2), 2)


def spread_rows(src, table, first, count):
    step = 256

    def one(i, carry):
        block = src[pl.ds(pl.multiple_of(i * step, step), step), :].astype(F32)
        at = 2 * first + i * (2 * step)
        table[pl.ds(pl.multiple_of(at, 8), step, stride=2), :] = block[:, :LANES]
        table[pl.ds(at + 1, step, stride=2), :] = block[:, LANES:]
        return carry

    lax.fori_loop(0, count // step, one, 0)


def class_places(cls, class_count, tile):
    rows = cls.shape[0]
    shift = rows.bit_length() - 1
    wide = class_count * rows
    member = jnp.concatenate([(cls == c).astype(F32) for c in range(class_count)], axis=0)
    member16 = member.astype(BF16)
    before = (iota2((LANES, LANES), 0) < iota2((LANES, LANES), 1)).astype(F32).astype(BF16)
    in_row = dot(member16, before)
    row_total = dot(member16, jnp.ones((LANES, LANES), BF16)).astype(BF16)
    a, b = iota2((wide, wide), 0), iota2((wide, wide), 1)
    same = (a >> shift) == (b >> shift)
    earlier_rows = jnp.logical_and(same, b < a).astype(F32).astype(BF16)
    row_start = dot(earlier_rows, row_total)
    class_total = dot(same.astype(F32).astype(BF16), row_total)
    tiles = ((class_total + (tile - 0.5)) * (1.0 / tile)).astype(I32).astype(F32)
    earlier = jnp.logical_and((b >> shift) < (a >> shift), (b & (rows - 1)) == 0)
    first_tile = dot(earlier.astype(F32).astype(BF16), tiles.astype(BF16))
    place = member * (first_tile * float(tile) + row_start + in_row)
    total = place[:rows]
    for c in range(1, class_count):
        total = total + place[c * rows:(c + 1) * rows]
    last_tile = (first_tile + tiles).astype(I32)
    lane = iota2((8, LANES), 1)
    tile_class = jnp.zeros((8, LANES), I32)
    for c in range(class_count - 1):
        tile_class = tile_class + (last_tile[c * rows:c * rows + 8] <= lane).astype(I32)
    tile_count = last_tile[wide - 8:]
    return (2.0 * total).astype(I32), tile_class, tile_count


def substeps(state, weights):
    bins = float(LANES)
    rows = state.shape[0] // 6
    pieces = [(state[p * rows:(p + 1) * rows, :LANES], state[p * rows:(p + 1) * rows, LANES:]) for p in range(6)]
    for _ in range(SUBSTEPS):
        operand = jnp.concatenate([jnp.concatenate(piece, axis=1).astype(BF16) for piece in pieces], axis=0)
        product = dot(operand, weights)
        for p, (one, two) in enumerate(pieces):
            here = product[p * rows:(p + 1) * rows]
            square_one = jnp.sum(one * one, axis=1, keepdims=True)
            square_two = jnp.sum(two * two, axis=1, keepdims=True)
            one = one + here[:, :LANES] * (1.0 / bins - pl.reciprocal(bins + square_one, approx=True))
            two = two + here[:, LANES:] * (1.0 / bins - pl.reciprocal(bins + square_two, approx=True))
            pieces[p] = (one, two)
    ones, twos = [piece[0] for piece in pieces], [piece[1] for piece in pieces]
    return jnp.concatenate(ones, axis=0).astype(BF16), jnp.concatenate(twos, axis=0).astype(BF16)


def send_rows(ids, steps, table, outbound, sent, sems, stages):
    span = LANES
    lines = ids.shape[0]

    def pull(line, stage):
        for j in range(span // GROUP):
            group = ids.at[line, pl.ds(j * GROUP, GROUP)]
            for k in range(GROUP):
                stage[rows2((j * GROUP + k) * 2), :] = table[rows2(group[steps[k]]), :]

    def push(block, i, stage):
        at = pl.ds(pl.multiple_of(i * span, span), span)
        block[at, 0:LANES] = stage[pl.ds(0, span, stride=2), :].astype(BF16)
        block[at, LANES:2 * LANES] = stage[pl.ds(1, span, stride=2), :].astype(BF16)

    pull(0, stages[0])
    first = 0
    copies = []
    for number, block in enumerate(outbound):
        spans = block.shape[0] // span

        def pair(i, carry):
            push(block, 2 * i, stages[0])
            pull(first + 2 * i + 1, stages[1])
            push(block, 2 * i + 1, stages[1])
            pull(jnp.minimum(first + 2 * i + 2, lines - 1), stages[0])
            return carry

        lax.fori_loop(0, spans // 2, pair, 0)
        first += spans
        copies.append(pltpu.make_async_copy(block, sent[number], sems.at[number]))
        copies[-1].start()
    for copy in copies:
        copy.wait()


def own_kernel(cells, cls_ref, exp_ref, dust_any, kern_any, out_any, any_up, any_down, any_left, any_right, out_up, out_down,
               out_left, out_right, send_sems, out, dust, kern, sorted_rows, weights, places_v, places, exp_v, exp_s, stage_a, stage_b, sem, dust_sems, kern_sem, exp_sem):
    class_count = kern.shape[0]
    rows = cells // LANES
    parts = dust_sems.shape[0]
    part = cells // parts
    kern_copy = pltpu.make_async_copy(kern_any, kern, kern_sem)
    kern_copy.start()
    dust_copies = []
    for p in range(parts):
        at = pl.ds(p * part, part)
        dust_copies.append(pltpu.make_async_copy(dust_any.at[at], dust.at[at], dust_sems.at[p]))
        dust_copies[-1].start()
    lines_of(exp_ref.at[0], exp_v, 2)
    exp_copy = pltpu.make_async_copy(exp_v, exp_s, exp_sem)
    exp_copy.start()
    place, tile_class, tile_count = class_places(cls_ref[...], class_count, TILE)
    places_v[0:rows, :] = place
    places_v[rows:rows + 8, :] = tile_class
    places_v[rows + 8:rows + 16, :] = tile_count
    copy = pltpu.make_async_copy(places_v, places, sem)
    copy.start()
    zero = jnp.zeros((LANES, LANES), BF16)
    kern_copy.wait()
    for c in range(class_count):
        for s in range(2):
            own = kern[c, s].astype(F32) * float(LANES)
            weights[c, s * LANES:(s + 1) * LANES, s * LANES:(s + 1) * LANES] = own.astype(BF16)
            weights[c, s * LANES:(s + 1) * LANES, (1 - s) * LANES:(2 - s) * LANES] = zero
    for dust_copy in dust_copies:
        dust_copy.wait()
    copy.wait()
    exp_copy.wait()
    steps = small_numbers(places[0, 0])

    def widen(r, stage):
        block = dust[pl.ds(pl.multiple_of(r * LANES, LANES), LANES), :].astype(F32)
        stage[pl.ds(0, LANES, stride=2), :] = block[:, :LANES]
        stage[pl.ds(1, LANES, stride=2), :] = block[:, LANES:]

    def scatter(r, stage):
        for j in range(LANES // GROUP):
            group = places.at[r, pl.ds(j * GROUP, GROUP)]
            for k in range(GROUP):
                sorted_rows[rows2(group[steps[k]]), :] = stage[rows2((j * GROUP + k) * 2), :]

    widen(0, stage_a)

    def pair(i, carry):
        scatter(2 * i, stage_a)
        widen(2 * i + 1, stage_b)
        scatter(2 * i + 1, stage_b)
        widen(jnp.minimum(2 * i + 2, rows - 1), stage_a)
        return carry

    lax.fori_loop(0, rows // 2, pair, 0)

    def tile(i, carry):
        first = i * (2 * TILE)
        at_one = pl.ds(pl.multiple_of(first, 8), TILE, stride=2)
        at_two = pl.ds(first + 1, TILE, stride=2)
        state = jnp.concatenate([sorted_rows[at_one, :], sorted_rows[at_two, :]], axis=1)
        one, two = substeps(state, weights[places[rows, i]])
        sorted_rows[at_one, :] = one.astype(F32)
        sorted_rows[at_two, :] = two.astype(F32)
        return carry

    lax.fori_loop(0, places[rows + 8, 0], tile, 0)

    def gather(r, carry):
        for j in range(LANES // GROUP):
            group = places.at[r, pl.ds(j * GROUP, GROUP)]
            for k in range(GROUP):
                at = (r * LANES + j * GROUP + k) * 2
                out[rows2(at), :] = sorted_rows[rows2(group[steps[k]]), :]
        return carry

    lax.fori_loop(0, rows, gather, 0)
    out_copy = pltpu.make_async_copy(out, out_any, sem)
    out_copy.start()
    send_rows(exp_s, steps, out, (out_up, out_down, out_left, out_right), (any_up, any_down, any_left, any_right), send_sems,
              (stage_a, stage_b))
    out_copy.wait()


def vmem():
    return pl.BlockSpec(memory_space=pltpu.VMEM)


def smem():
    return pl.BlockSpec(memory_space=pltpu.SMEM)


def anywhere():
    return pl.BlockSpec(memory_space=pl.ANY)


def hbm():
    return pl.BlockSpec(memory_space=pltpu.HBM)


def own_cells(dust, classes, kernels, export_ids):
    cells = dust.shape[0]
    export = export_ids.shape[2]
    rows = cells // LANES
    class_count = kernels.shape[0]
    most = cells // TILE + class_count
    block = jax.ShapeDtypeStruct((export, 2 * LANES), BF16)
    return pl.pallas_call(
        functools.partial(own_kernel, cells),
        out_shape=(jax.ShapeDtypeStruct((2 * cells, LANES), F32), block, block, block, block),
        in_specs=[vmem(), vmem(), hbm(), hbm()],
        out_specs=(hbm(), hbm(), hbm(), hbm(), hbm()),
        scratch_shapes=[
            pltpu.VMEM(block.shape, BF16),
            pltpu.VMEM(block.shape, BF16),
            pltpu.VMEM(block.shape, BF16),
            pltpu.VMEM(block.shape, BF16),
            pltpu.SemaphoreType.DMA((4,)),
            pltpu.VMEM((2 * cells, LANES), F32),
            pltpu.VMEM((cells, 2 * LANES), BF16),
            pltpu.VMEM(kernels.shape, BF16),
            pltpu.VMEM((2 * most * TILE + 8, LANES), F32),
            pltpu.VMEM((class_count, 2 * LANES, 2 * LANES), BF16),
            pltpu.VMEM((rows + 16, LANES), I32),
            pltpu.SMEM((rows + 16, LANES), I32),
            pltpu.VMEM((4 * export // LANES, LANES), I32),
            pltpu.SMEM((4 * export // LANES, LANES), I32),
            pltpu.VMEM((2 * LANES + 8, LANES), F32),
            pltpu.VMEM((2 * LANES + 8, LANES), F32),
            pltpu.SemaphoreType.DMA,
            pltpu.SemaphoreType.DMA((4,)),
            pltpu.SemaphoreType.DMA,
            pltpu.SemaphoreType.DMA,
        ],
        compiler_params=pltpu.CompilerParams(vmem_limit_bytes=VMEM_KIB * KIB),
        cost_estimate=pl.CostEstimate(flops=9_000_000_000, bytes_accessed=12 * MIB, transcendentals=0),
        name="coagulate_own",
    )(classes.reshape(rows, LANES), export_ids, dust, kernels)


def pairs(start):
    return pl.ds(pl.multiple_of(start, 8), CHUNK, stride=2), pl.ds(start + 1, CHUNK, stride=2)


def face_sums(own_one, own_two, weights, stage, face_count):
    one, two = own_one, own_two
    for f in range(face_count):
        c = jnp.broadcast_to(weights[:, f:f + 1], (CHUNK, LANES))
        one = one + c * (stage[pl.ds(2 * f * CHUNK, CHUNK, stride=2), :] - own_one)
        two = two + c * (stage[pl.ds(2 * f * CHUNK + 1, CHUNK, stride=2), :] - own_two)
    return one, two


def turn_columns(coef, late, both, columns):
    together = 2
    padded = both.shape[0] // 2
    both[0:coef.shape[0], :] = coef[...]
    both[padded:padded + coef.shape[0], :] = late

    def turn(b, carry):
        for u in range(together):
            at = pl.ds(pl.multiple_of((b * together + u) * LANES, LANES), LANES)
            columns[at, :] = both[:, at].T
        return carry

    lax.fori_loop(0, columns.shape[0] // (LANES * together), turn, 0)


def start_faces(faces, faces_v, faces_s, sems):
    lines_of(faces, faces_v, 2)
    per_face = faces.shape[1] // LANES
    parts = sems.shape[0]
    copies = []
    for p in range(parts):
        copies.append([])
        for f in range(faces.shape[0]):
            at = pl.ds(f * per_face + p * (per_face // parts), per_face // parts)
            copies[p].append(pltpu.make_async_copy(faces_v.at[at], faces_s.at[at], sems.at[p, f]))
            copies[p][f].start()
    return copies


def start_ghosts(ghosts, landed, sems):
    copies = []
    for k, ghost in enumerate(ghosts):
        copies.append(pltpu.make_async_copy(ghost, landed.at[k], sems.at[k]))
        copies[-1].start()
    return copies


def spread_ghosts(copies, landed, table, first):
    for k, copy in enumerate(copies):
        copy.wait()
        spread_rows(landed.at[k], table, first + k * landed.shape[1], landed.shape[1])


def late_lists(face_count, cells, out, out_coef, counts, lines, coef_lines):
    per_face = cells // LANES
    every = face_count * per_face
    shift = per_face.bit_length() - 1
    to = lines[...]
    late = (to >= 2 * cells).astype(F32)
    late16 = late.astype(BF16)
    before = (iota2((LANES, LANES), 0) < iota2((LANES, LANES), 1)).astype(F32).astype(BF16)
    line_total = dot(late16, jnp.ones((LANES, LANES), BF16)).astype(BF16)
    a, b = iota2((every, every), 0), iota2((every, every), 1)
    earlier = jnp.logical_and((a >> shift) == (b >> shift), b < a).astype(F32).astype(BF16)
    line_start = dot(earlier, line_total)
    rank = (dot(late16, before) + line_start).astype(I32)
    place = (iota2((every, LANES), 0) & (per_face - 1)) * LANES + iota2((every, LANES), 1)
    ahead = jnp.where(to >= 2 * cells, place - rank, 0)
    lane = iota2((per_face, LANES), 1)
    where = iota2((per_face, LANES), 0) * LANES + lane

    def from_right(x, digit):
        if digit >= 7:
            return pltpu.roll(x, per_face - (1 << (digit - 7)), 0)
        near = pltpu.roll(x, LANES - (1 << digit), 1)
        return jnp.where(lane < LANES - (1 << digit), near, pltpu.roll(near, per_face - 1, 0))

    for f in range(face_count):
        at = slice(f * per_face, (f + 1) * per_face)
        last = (f + 1) * per_face - 1
        number = (line_start[last:last + 1, :] + line_total[last:last + 1, :].astype(F32)).astype(I32)
        counts[f:f + 1, :] = number
        word = (where << 14) + (to[at] - 2 * cells)
        move = ahead[at]
        weight = coef_lines[at]
        for digit in range(cells.bit_length() - 1):
            next_word, next_move = from_right(word, digit), from_right(move, digit)
            takes = ((next_move >> digit) & 1) == 1
            word = jnp.where(takes, next_word, word)
            weight = jnp.where(takes, from_right(weight, digit), weight)
            move = jnp.where(takes, next_move, jnp.where(((move >> digit) & 1) == 1, 0, move))
        used = where < number
        of_cells = jnp.where(used, (word >> 14) * 2, 2 * cells)
        out_coef[at, :] = jnp.where(used, weight, 0.0)
        of_rows = jnp.where(used, word & ((1 << 14) - 1), 0)
        start = 2 * f * per_face
        rest = per_face - FIRST_LINES
        out[start:start + FIRST_LINES, :] = of_cells[:FIRST_LINES]
        out[start + FIRST_LINES:start + 2 * FIRST_LINES, :] = of_rows[:FIRST_LINES]
        out[start + 2 * FIRST_LINES:start + 2 * FIRST_LINES + rest, :] = of_cells[FIRST_LINES:]
        out[start + 2 * FIRST_LINES + rest:start + 2 * per_face, :] = of_rows[FIRST_LINES:]


def early_kernel(face_count, cells, late_rows, faces_any, mig, mig_counts, own, coef_any, out_any, mig_sums, mig_coef, mig_late, lists,
                 list_coef, counts, out, faces, coef, coef_v, input_sems, table,
                 stage_a, stage_b, both, columns, faces_v, faces_s, sem, face_sem, out_sems):
    inputs = [pltpu.make_async_copy(faces_any, faces, input_sems.at[0]), pltpu.make_async_copy(coef_any, coef, input_sems.at[1])]
    for one in inputs:
        one.start()
    copy = pltpu.make_async_copy(own, table.at[pl.ds(0, 2 * cells)], sem)
    copy.start()
    for one in inputs:
        one.wait()
    face_copies = start_faces(faces, faces_v, faces_s, face_sem)

    def clear(i, carry):
        table[pl.ds(pl.multiple_of(2 * cells + i * 256, 256), 256), :] = jnp.zeros((256, LANES), F32)
        return carry

    lax.fori_loop(0, 2 * late_rows // 256, clear, 0)
    turn_columns(coef, jnp.where(faces[...] >= cells, 2 * (faces[...] - cells), 2 * late_rows).astype(F32), both, columns)
    lines_of(coef, coef_v, 1.0)
    late_lists(face_count, cells, lists, list_coef, counts, faces_v, coef_v)
    for part in face_copies[0]:
        part.wait()
    flat = faces_s.reshape(face_count * cells)
    steps = small_numbers(faces_s[0, 0])
    copy.wait()

    def pull(i, stage):
        for f in range(face_count):
            for j in range(CHUNK // GROUP):
                group = flat.at[pl.ds(i * CHUNK + (f * cells + j * GROUP), GROUP)]
                for k in range(GROUP):
                    stage[rows2((f * CHUNK + j * GROUP + k) * 2), :] = table[rows2(group[steps[k]]), :]

    def push(i, stage):
        at = pairs(i * (2 * CHUNK))
        weights = columns[pl.ds(pl.multiple_of(i * CHUNK, CHUNK), CHUNK), :]
        one, two = face_sums(table[at[0], :], table[at[1], :], weights, stage, face_count)
        out[at[0], :] = one
        out[at[1], :] = two

    pull(0, stage_a)
    chunks = cells // CHUNK

    def pair(i, carry):
        push(2 * i, stage_a)
        pull(2 * i + 1, stage_b)
        push(2 * i + 1, stage_b)
        pull(jnp.minimum(2 * i + 2, chunks - 1), stage_a)
        return carry

    parts = out_sems.shape[0]
    done = []
    for p in range(parts):
        if p + 1 < parts:
            for part in face_copies[p + 1]:
                part.wait()
        lax.fori_loop(p * (chunks // 2 // parts), (p + 1) * (chunks // 2 // parts), pair, 0)
        at = pl.ds(p * (2 * cells // parts), 2 * cells // parts)
        done.append(pltpu.make_async_copy(out.at[at], out_any.at[at], out_sems.at[p]))
        done[-1].start()

    def leaving(i, carry):
        for u in range(CHUNK):
            cell = mig[u, i]
            at = i * CHUNK + u
            mig_sums[rows2(2 * at), :] = out[rows2(2 * cell), :]
            mig_coef[pl.ds(at, 1), :] = columns[pl.ds(cell, 1), :]
        return carry

    lax.fori_loop(0, mig.shape[1], leaving, 0)
    lines = mig_coef.shape[0] // LANES
    padded = both.shape[0] // 2
    for i in range(lines):
        turned = mig_coef[i * LANES:(i + 1) * LANES, :].T.astype(I32)
        for f in range(face_count):
            mig_late[f * lines + i:f * lines + i + 1, :] = turned[padded + f:padded + f + 1, :]
    last = face_count * lines
    mig_late[last:last + 1, 0:mig_counts.shape[1]] = mig_counts[...]
    for part in done:
        part.wait()


def diffuse_early(faces, mig, counts, own, coef, late_rows):
    face_count, cells = coef.shape
    padded = face_count + -face_count % 8
    leaving = mig.shape[0] * mig.shape[1]
    return pl.pallas_call(
        functools.partial(early_kernel, face_count, cells, late_rows),
        out_shape=(
            jax.ShapeDtypeStruct((2 * cells, LANES), F32),
            jax.ShapeDtypeStruct((2 * leaving, LANES), F32),
            jax.ShapeDtypeStruct((leaving, 2 * padded), F32),
            jax.ShapeDtypeStruct((face_count * leaving // LANES + 8, LANES), I32),
            jax.ShapeDtypeStruct((2 * face_count * cells // LANES, LANES), I32),
            jax.ShapeDtypeStruct((face_count * cells // LANES, LANES), F32),
            jax.ShapeDtypeStruct((8, LANES), I32),
        ),
        in_specs=[hbm(), smem(), vmem(), hbm(), hbm()],
        out_specs=(hbm(), vmem(), vmem(), vmem(), vmem(), vmem(), vmem()),
        scratch_shapes=[
            pltpu.VMEM((2 * cells + 8, LANES), F32),
            pltpu.VMEM((face_count, cells), I32),
            pltpu.VMEM((face_count, cells), F32),
            pltpu.VMEM((face_count * cells // LANES, LANES), F32),
            pltpu.SemaphoreType.DMA((2,)),
            pltpu.VMEM((2 * (cells + late_rows), LANES), F32),
            pltpu.VMEM((2 * face_count * CHUNK + 8, LANES), F32),
            pltpu.VMEM((2 * face_count * CHUNK + 8, LANES), F32),
            pltpu.VMEM((2 * padded, cells), F32),
            pltpu.VMEM((cells, 2 * padded), F32),
            pltpu.VMEM((face_count * cells // LANES, LANES), I32),
            pltpu.SMEM((face_count * cells // LANES, LANES), I32),
            pltpu.SemaphoreType.DMA,
            pltpu.SemaphoreType.DMA((4, face_count)),
            pltpu.SemaphoreType.DMA((4,)),
        ],
        compiler_params=pltpu.CompilerParams(vmem_limit_bytes=VMEM_KIB * KIB),
        cost_estimate=pl.CostEstimate(flops=20_000_000_000, bytes_accessed=16 * MIB, transcendentals=0),
        name="diffuse_early",
    )(faces, mig, counts, own, coef)


def leave_kernel(face_count, late_any, sums_any, coef_any, g0, g1, g2, g3, out, table, landed, stage_a, stage_b,
                 late_s, mig_sums, mig_coef, late_sem, sums_sem, coef_sem, ghost_sems):
    ghost_copies = start_ghosts((g0, g1, g2, g3), landed, ghost_sems)
    copies = [
        pltpu.make_async_copy(late_any, late_s, late_sem),
        pltpu.make_async_copy(sums_any, mig_sums.at[pl.ds(0, sums_any.shape[0])], sums_sem),
        pltpu.make_async_copy(coef_any, mig_coef, coef_sem),
    ]
    for copy in copies:
        copy.start()
    ghost_rows = landed.shape[0] * landed.shape[1]
    table[2 * ghost_rows:2 * ghost_rows + 8, :] = jnp.zeros((8, LANES), F32)
    spread_ghosts(ghost_copies, landed, table, 0)
    for copy in copies:
        copy.wait()
    cells = out.shape[0]
    mig_late = late_s.reshape(late_s.shape[0] * LANES)
    steps = small_numbers(late_s[0, 0])
    chunks = cells // CHUNK

    def pull(i, stage):
        for f in range(face_count):
            for j in range(CHUNK // GROUP):
                group = mig_late.at[pl.ds(i * CHUNK + (f * cells + j * GROUP), GROUP)]
                for k in range(GROUP):
                    stage[rows2((f * CHUNK + j * GROUP + k) * 2), :] = table[rows2(group[steps[k]]), :]

    def push(i, stage):
        at = pairs(i * (2 * CHUNK))
        here = pl.ds(pl.multiple_of(i * CHUNK, CHUNK), CHUNK)
        one, two = mig_sums[at[0], :], mig_sums[at[1], :]
        weights = mig_coef[here, :]
        for f in range(face_count):
            c = jnp.broadcast_to(weights[:, f:f + 1], (CHUNK, LANES))
            one = one + c * stage[pl.ds(2 * f * CHUNK, CHUNK, stride=2), :]
            two = two + c * stage[pl.ds(2 * f * CHUNK + 1, CHUNK, stride=2), :]
        keep = iota2((CHUNK, LANES), 0) < mig_late[face_count * cells + i]
        out[here, 0:LANES] = jnp.where(keep, one, 0.0).astype(BF16)
        out[here, LANES:2 * LANES] = jnp.where(keep, two, 0.0).astype(BF16)

    pull(0, stage_a)

    def pair(i, carry):
        push(2 * i, stage_a)
        pull(2 * i + 1, stage_b)
        push(2 * i + 1, stage_b)
        pull(jnp.minimum(2 * i + 2, chunks - 1), stage_a)
        return carry

    lax.fori_loop(0, chunks // 2, pair, 0)


def diffuse_leaving(mig_late, mig_sums, mig_coef, ghosts, face_count):
    ghost_rows = sum(g.shape[0] for g in ghosts)
    return pl.pallas_call(
        functools.partial(leave_kernel, face_count),
        out_shape=jax.ShapeDtypeStruct((mig_coef.shape[0], 2 * LANES), BF16),
        in_specs=[anywhere()] * 7,
        out_specs=vmem(),
        scratch_shapes=[
            pltpu.VMEM((2 * ghost_rows + 8, LANES), F32),
            pltpu.VMEM((len(ghosts),) + ghosts[0].shape, BF16),
            pltpu.VMEM((2 * face_count * CHUNK + 8, LANES), F32),
            pltpu.VMEM((2 * face_count * CHUNK + 8, LANES), F32),
            pltpu.SMEM(mig_late.shape, I32),
            pltpu.VMEM((mig_sums.shape[0] + 8, LANES), F32),
            pltpu.VMEM(mig_coef.shape, F32),
            pltpu.SemaphoreType.DMA,
            pltpu.SemaphoreType.DMA,
            pltpu.SemaphoreType.DMA,
            pltpu.SemaphoreType.DMA((len(ghosts),)),
        ],
        compiler_params=pltpu.CompilerParams(vmem_limit_bytes=VMEM_KIB * KIB),
        cost_estimate=pl.CostEstimate(flops=500_000_000, bytes_accessed=8 * MIB, transcendentals=0),
        name="diffuse_leaving",
    )(mig_late, mig_sums, mig_coef, *ghosts)


def late_kernel(face_count, cells, lists, list_coef, counts, early, g0, g1, g2, g3, out_any, out, sums, table, landed, lists_s,
                coef_s, counts_s, sem, ghost_sems, coef_sems, list_sems, count_sem, out_sems):
    ghost_copies = start_ghosts((g0, g1, g2, g3), landed, ghost_sems)
    copy = pltpu.make_async_copy(early, sums.at[pl.ds(0, 2 * cells)], sem)
    copy.start()
    count_copy = pltpu.make_async_copy(counts, counts_s, count_sem)
    count_copy.start()
    list_copies = []
    for f in range(face_count):
        first = pl.ds(2 * f * cells // LANES, 2 * FIRST_LINES)
        part = pltpu.make_async_copy(lists.at[first], lists_s.at[f, pl.ds(0, 2 * FIRST_LINES)], list_sems.at[f])
        part.start()
        list_copies.append(part)
        first = pl.ds(f * cells // LANES, 2 * FIRST_LINES)
        part = pltpu.make_async_copy(list_coef.at[first], coef_s.at[f, pl.ds(0, 2 * FIRST_LINES)], coef_sems.at[f])
        part.start()
        list_copies.append(part)
    spread_ghosts(ghost_copies, landed, table, 0)
    count_copy.wait()
    steps = small_numbers(counts_s[0, 0])
    for part in list_copies:
        part.wait()
    copy.wait()
    flat_lists = lists_s.reshape(face_count * 2 * cells)
    flat_coef = coef_s.reshape(face_count * cells)
    for f in range(face_count):
        number = counts_s[f, 0]

        per_line = LANES // BATCH
        split = FIRST_LINES * per_line
        rest = 2 * cells // LANES - 2 * FIRST_LINES

        def add(cell_at, row_at, coef_at):
            for j in range(BATCH // GROUP):
                found = []
                of_cells = flat_lists.at[pl.ds(cell_at + j * GROUP, GROUP)]
                of_rows = flat_lists.at[pl.ds(row_at + j * GROUP, GROUP)]
                weights = flat_coef.at[pl.ds(coef_at + j * GROUP, GROUP)]
                for k in range(GROUP):
                    row = rows2(of_cells[steps[k]])
                    late = table[rows2(of_rows[steps[k]]), :]
                    found.append((row, sums[row, :] + weights[steps[k]] * late))
                for row, value in found:
                    sums[row, :] = value

        def near(i, carry):
            at = i * BATCH
            add(at + f * 2 * cells, at + (f * 2 * cells + FIRST_LINES * LANES), at + f * cells)
            return carry

        def far(i, carry):
            at = i * BATCH
            add(at + (f * 2 * cells + FIRST_LINES * LANES), at + (f * 2 * cells + cells), at + f * cells)
            return carry

        batches = (number + (BATCH - 1)) // BATCH
        lax.fori_loop(0, jnp.minimum(batches, split), near, 0)

        @pl.when(batches > split)
        def _():
            at = pl.ds(2 * f * cells // LANES + 2 * FIRST_LINES, rest)
            more = pltpu.make_async_copy(lists.at[at], lists_s.at[f, pl.ds(2 * FIRST_LINES, rest)], list_sems.at[f])
            more.start()
            more.wait()
            rest_coef = cells // LANES - 2 * FIRST_LINES
            at = pl.ds(f * cells // LANES + 2 * FIRST_LINES, rest_coef)
            more = pltpu.make_async_copy(list_coef.at[at], coef_s.at[f, pl.ds(2 * FIRST_LINES, rest_coef)], coef_sems.at[f])
            more.start()
            more.wait()
            lax.fori_loop(split, batches, far, 0)

    span = 256

    def pack(i, carry):
        at = pl.ds(pl.multiple_of(i * span, span), span)
        out[at, 0:LANES] = sums[pl.ds(pl.multiple_of(i * 2 * span, span), span, stride=2), :].astype(BF16)
        out[at, LANES:2 * LANES] = sums[pl.ds(i * 2 * span + 1, span, stride=2), :].astype(BF16)
        return carry

    parts = out_sems.shape[0]
    spans = cells // span // parts
    done = []
    for p in range(parts):
        lax.fori_loop(p * spans, (p + 1) * spans, pack, 0)
        at = pl.ds(p * (cells // parts), cells // parts)
        done.append(pltpu.make_async_copy(out.at[at], out_any.at[at], out_sems.at[p]))
        done[-1].start()
    for part in done:
        part.wait()


def diffuse_late(lists, list_coef, counts, early, ghosts, face_count):
    cells = early.shape[0] // 2
    ghost_rows = sum(g.shape[0] for g in ghosts)
    return pl.pallas_call(
        functools.partial(late_kernel, face_count, cells),
        out_shape=jax.ShapeDtypeStruct((cells, 2 * LANES), BF16),
        in_specs=[hbm(), hbm(), hbm(), hbm()] + [anywhere()] * len(ghosts),
        out_specs=hbm(),
        scratch_shapes=[
            pltpu.VMEM((cells, 2 * LANES), BF16),
            pltpu.VMEM((2 * cells + 16, LANES), F32),
            pltpu.VMEM((2 * ghost_rows + 8, LANES), F32),
            pltpu.VMEM((len(ghosts),) + ghosts[0].shape, BF16),
            pltpu.SMEM((face_count, 2 * cells // LANES, LANES), I32),
            pltpu.SMEM((face_count, cells // LANES, LANES), F32),
            pltpu.SMEM((8, LANES), I32),
            pltpu.SemaphoreType.DMA,
            pltpu.SemaphoreType.DMA((len(ghosts),)),
            pltpu.SemaphoreType.DMA((face_count,)),
            pltpu.SemaphoreType.DMA((face_count,)),
            pltpu.SemaphoreType.DMA,
            pltpu.SemaphoreType.DMA((8,)),
        ],
        compiler_params=pltpu.CompilerParams(vmem_limit_bytes=LESS_VMEM_KIB * KIB),
        cost_estimate=pl.CostEstimate(flops=9_000_000_000, bytes_accessed=24 * MIB, transcendentals=0),
        name="diffuse_late",
    )(lists, list_coef, counts, early, *ghosts)


def body(dust, classes, kernels, export_ids, faces, face_coef, mig_ids, mig_counts):
    row_width = dust.shape[1]
    export = export_ids.shape[2]
    domains = mig_counts.shape[1]
    capacity = mig_ids.shape[1]
    own, up, down, left, right = own_cells(dust, classes, kernels, export_ids)
    g0, g1 = passed_along(up, "dx", 1), passed_along(down, "dx", -1)
    g2, g3 = passed_along(left, "dy", 1), passed_along(right, "dy", -1)
    ghosts = (g0, g1, g2, g3)
    faces, face_coef, mig_ids, own = lax.optimization_barrier((faces, face_coef, mig_ids, own))
    mig = mig_ids.T
    early, mig_sums, mig_coef, mig_late, lists, list_coef, list_counts = diffuse_early(faces, mig, mig_counts, own, face_coef, 4 * export)
    leaving = diffuse_leaving(mig_late, mig_sums, mig_coef, ghosts, face_coef.shape[0])
    arrived = lax.all_to_all(leaving.reshape(domains, capacity, row_width), ("dx", "dy"), split_axis=0, concat_axis=0, tiled=True)
    updated = diffuse_late(lists, list_coef, list_counts, early, ghosts, face_coef.shape[0])
    return (updated, arrived.reshape(domains * capacity, row_width))


def solution(mesh):
    return jax.shard_map(
        body,
        mesh=mesh,
        in_specs=(
            P(("dx", "dy"), None),
            P(("dx", "dy")),
            P(),
            P(("dx", "dy"), None, None),
            P(None, ("dx", "dy")),
            P(None, ("dx", "dy")),
            P(("dx", "dy"), None),
            P(("dx", "dy"), None),
        ),
        out_specs=(P(("dx", "dy"), None), P(("dx", "dy"), None)),
        check_vma=False,
    )
```
